256 devices in a mesh: seq: 16 (over y, x), head: 16 (over z, core).
Axes of the slice: x: 4, y: 4, z: 8, core: 2. Of those that a mesh axis runs over, the one named last changes fastest.
Arguments:
- queries: bfloat16 [16384, 4096], P('seq', 'head'), may hold values from -6 to 6
- key_states: bfloat16 [16384, 4096], P('seq', 'head'), may hold values from -6 to 6
- values: bfloat16 [16384, 4096], P('seq', 'head'), may hold values from -6 to 6
- selection: int32 [32, 32, 4], P('head', 'seq'), may hold values from 0 to 31, as said below
- out_weight: bfloat16 [4096, 2048], P('head'), may hold values from -0.09375 to 0.09375
- cotangent: bfloat16 [16384, 2048], P('seq'), may hold values from -6 to 6
Outputs:
- projected: bfloat16 [16384, 2048], P(('seq', 'head'))
- query_grad: bfloat16 [16384, 4096], P('seq', 'head')
- key_grad: bfloat16 [16384, 4096], P('seq', 'head')
- value_grad: bfloat16 [16384, 4096], P('seq', 'head')
- weight_grad: float32 [4096, 2048], P('head', 'seq')
The draws below stay inside these ranges and needn't reach their ends.
Inputs may be any that keep to these rules, and one draw needn't show every extreme that they name: Entry selection[h, b, t] is either a block below b, the entries of one row distinct, or b itself, which chooses nothing; a row holds b only where fewer than 4 blocks are chosen. For each head, the blocks chosen by the 2 query blocks of one index of seq that lie on one other index of seq are one block at most.
All inputs are finite; a program needn't handle non-finite values.
Results may differ from the reference program's by a relative error of at most 0.022.
Values may be sent and summed in bfloat16 or wider, within the bound.
A program may use at most 192 MiB of HBM per device.

```python
import math
import jax
import jax.numpy as jnp
from jax import lax

H = 32
HD = 128
BLOCK = 512
TOPK = 4
DOUT = 2048
TOK_DEV = 1024
HP = 2
QBD = 2
TOKENS = 16384
NB = 32
N_SEQ = 16
N_HEAD = 16


def draw_queries(key, part):
    key = jax.random.fold_in(key, 5)
    return jnp.clip(jax.random.normal(key, (TOKENS, H * HD), jnp.float32), -6.0, 6.0).astype(jnp.bfloat16)


def draw_key_states(key, part):
    key = jax.random.fold_in(key, 6)
    return jnp.clip(jax.random.normal(key, (TOKENS, H * HD), jnp.float32), -6.0, 6.0).astype(jnp.bfloat16)


def draw_selection(key, part):
    key = jax.random.fold_in(key, 7)
    key_one, key_two, key_three = jax.random.split(key, 3)
    per_device = TOK_DEV // BLOCK
    seq_total = NB // per_device
    owner_ids = jnp.arange(NB, dtype=jnp.int32) // per_device
    local_ids = jnp.arange(NB, dtype=jnp.int32) % per_device
    blocks_query = jnp.arange(NB, dtype=jnp.int32)[:, None]
    blocks_key = jnp.arange(NB, dtype=jnp.int32)[None, :]
    popular = (jax.random.randint(key_one, (H, seq_total), 0, 4) == 0).astype(jnp.int32)
    designated = jax.random.randint(key_two, (H, seq_total, seq_total), 0, per_device)
    picks = designated[:, owner_ids][:, :, owner_ids]
    remote_ok = (owner_ids[None, :] < owner_ids[:, None])[None] & (picks == local_ids[None, None, :])
    local_ok = ((owner_ids[None, :] == owner_ids[:, None]) & (blocks_key < blocks_query))[None]
    candidate = remote_ok | local_ok
    matching = (owner_ids[None, :] % per_device == local_ids[:, None] % per_device)[None] & remote_ok
    jitter = jax.random.randint(key_three, (H, NB, NB), 0, 1000)
    scores = (jitter + 3000 * popular[:, owner_ids][:, None, :] + 10000 * matching.astype(jnp.int32)) * NB + blocks_key[None]
    scores = jnp.where(candidate, scores, -1 - blocks_key[None])
    top_values, top_index = lax.top_k(scores, TOPK)
    return jnp.where(top_values >= 0, top_index, blocks_query[None]).astype(jnp.int32)


def with_spikes(values, stream_key, source, target, shards_of, factor):
    owner, partner = [(jnp.arange(values.shape[axis_at]) // (values.shape[axis_at] // shards_of)).reshape([-1 if axis == axis_at else 1 for axis in range(values.ndim)]) for axis_at in (source, target)]
    chosen = jax.random.permutation(stream_key, shards_of)[partner]
    strong = (owner == chosen) | (owner == (partner + shards_of // 2) % shards_of)
    return jnp.where(strong, factor * values, values)


def shard_levels(rng, dims, cuts, least, largest):
    def one(dim, parts):
        steps = jax.random.uniform(jax.random.fold_in(jax.random.fold_in(rng, 6), dim), (parts,), jnp.float32, least / len(cuts), largest / len(cuts))
        return jnp.repeat(jnp.exp(steps), dims[dim] // parts).reshape((-1,) + (1,) * (len(dims) - dim - 1))

    loudness = one(*cuts[0])
    for cut in cuts[1:]:
        loudness = loudness * one(*cut)
    return loudness


def bell_draw(own_key, shape, scale, bound, pieces=(), kind=jnp.bfloat16):
    drawn = scale * jax.random.normal(own_key, shape, jnp.float32)
    if pieces:
        drawn = drawn * shard_levels(own_key, shape, pieces, -0.22, 0.18)
    return jnp.clip(drawn, -bound, bound).astype(kind)


def gaussian_with(own_key, shape, spread, most, shards, heavy, kind=jnp.bfloat16):
    drawn = spread * jax.random.normal(own_key, shape, jnp.float32)
    if shards:
        drawn = drawn * shard_levels(own_key, shape, shards, -0.22, 0.18)
    return jnp.clip(with_spikes(drawn, jax.random.fold_in(own_key, 3), *heavy), -most, most).astype(kind)


def setup_inputs(seed: int = 0) -> dict:
    arg_keys = jax.random.split(jax.random.key(seed), 7)
    queries = draw_queries(jax.random.fold_in(arg_keys[6], 71), 0)
    key_states = draw_key_states(jax.random.fold_in(arg_keys[6], 71), 0)
    values = bell_draw(arg_keys[2], (TOKENS, H * HD), 1.0, 6.0, ((0, 16), (1, 16)))
    selection = draw_selection(jax.random.fold_in(arg_keys[6], 71), 0)
    out_weight = bell_draw(arg_keys[4], (H * HD, DOUT), (H * HD) ** -0.5, 0.09375, ((0, 16),))
    cotangent = gaussian_with(arg_keys[5], (TOKENS, DOUT), 1.0, 6.0, ((0, 16),), (0, 1, 16, 2.0))
    return dict(queries=queries, key_states=key_states, values=values, selection=selection, out_weight=out_weight, cotangent=cotangent)


def allowed_keys(usable):
    columns = (TOPK + 1) * BLOCK
    row_ids = lax.broadcasted_iota(jnp.int32, (BLOCK, columns), 0)
    col_ids = lax.broadcasted_iota(jnp.int32, (BLOCK, columns), 1)
    causal = (col_ids < BLOCK) & (col_ids <= row_ids)
    extended = jnp.concatenate([jnp.zeros((1,), jnp.bool_), usable])
    picked = jnp.repeat(extended, BLOCK)[None, :]
    return causal | picked

def softmax_weights(query_rows, key_rows, allowed):
    scaling = 1.0 / math.sqrt(HD)
    scores = jnp.einsum('qd,kd->qk', query_rows.astype(jnp.float32), key_rows.astype(jnp.float32)) * scaling
    scores = jnp.where(allowed, scores, -1e+30)
    row_max = lax.optimization_barrier(jnp.max(scores, axis=1, keepdims=True))
    expons = jnp.exp(scores - row_max)
    return expons / lax.optimization_barrier(jnp.sum(expons, axis=1, keepdims=True))

def head_sets(h_index, queries, key_states, values, selection):
    column = h_index * HD
    query_blocks = lax.dynamic_slice_in_dim(queries, column, HD, 1).reshape(NB, BLOCK, HD)
    key_blocks = lax.dynamic_slice_in_dim(key_states, column, HD, 1).reshape(NB, BLOCK, HD)
    value_blocks = lax.dynamic_slice_in_dim(values, column, HD, 1).reshape(NB, BLOCK, HD)
    chosen_ids = lax.dynamic_index_in_dim(selection, h_index, 0, keepdims=False).astype(jnp.int32)
    key_sets = jnp.concatenate([key_blocks[:, None], key_blocks[chosen_ids]], axis=1).reshape(NB, (TOPK + 1) * BLOCK, HD)
    value_sets = jnp.concatenate([value_blocks[:, None], value_blocks[chosen_ids]], axis=1).reshape(NB, (TOPK + 1) * BLOCK, HD)
    usable = chosen_ids < jnp.arange(NB, dtype=jnp.int32)[:, None]
    return (query_blocks, key_sets, value_sets, usable, chosen_ids)

def reference(queries, key_states, values, selection, out_weight, cotangent):
    scaling = 1.0 / math.sqrt(HD)

    def forward_head(h_index):
        query_blocks, key_sets, value_sets, usable, chosen_ids = head_sets(h_index, queries, key_states, values, selection)

        def one_block(query_rows, key_rows, value_rows, usable_row):
            weights = softmax_weights(query_rows, key_rows, allowed_keys(usable_row))
            weights_bf = lax.optimization_barrier(weights.astype(jnp.bfloat16)).astype(jnp.float32)
            return jnp.einsum('qk,kd->qd', weights_bf, value_rows.astype(jnp.float32)).astype(jnp.bfloat16)
        return jax.vmap(one_block)(query_blocks, key_sets, value_sets, usable)
    attn_heads = lax.map(forward_head, jnp.arange(H, dtype=jnp.int32))
    attention = attn_heads.transpose(1, 2, 0, 3).reshape(TOKENS, H * HD)
    grouped_attn = attention.reshape(TOKENS, N_HEAD, HP * HD)
    weight_groups = out_weight.reshape(N_HEAD, HP * HD, DOUT)

    def add_group(carry, group_id):
        slab_attn = lax.dynamic_index_in_dim(grouped_attn, group_id, 1, keepdims=False)
        slab_weight = lax.dynamic_index_in_dim(weight_groups, group_id, 0, keepdims=False)
        partial_sum = jnp.dot(slab_attn, slab_weight, preferred_element_type=jnp.float32)
        rounded = lax.optimization_barrier(partial_sum.astype(jnp.bfloat16))
        return (carry + rounded.astype(jnp.float32), None)
    summed, _ = lax.scan(add_group, jnp.zeros((TOKENS, DOUT), jnp.float32), jnp.arange(N_HEAD, dtype=jnp.int32))
    projected = summed.astype(jnp.bfloat16)
    grad_attn = jnp.dot(cotangent, out_weight.T, preferred_element_type=jnp.float32).astype(jnp.bfloat16)
    weight_grad = jnp.dot(attention.T, cotangent, preferred_element_type=jnp.float32)
    owner_of = jnp.arange(NB, dtype=jnp.int32) // QBD

    def backward_head(packed):
        h_index, attn_blocks = packed
        query_blocks, key_sets, value_sets, usable, chosen_ids = head_sets(h_index, queries, key_states, values, selection)
        grad_blocks = lax.dynamic_slice_in_dim(grad_attn, h_index * HD, HD, 1).reshape(NB, BLOCK, HD)

        def one_block(query_rows, key_rows, value_rows, usable_row, grad_rows, attn_rows):
            weights = softmax_weights(query_rows, key_rows, allowed_keys(usable_row))
            weights_bf = lax.optimization_barrier(weights.astype(jnp.bfloat16)).astype(jnp.float32)
            grad_float = grad_rows.astype(jnp.float32)
            grad_weights = jnp.einsum('qd,kd->qk', grad_float, value_rows.astype(jnp.float32))
            row_delta = lax.optimization_barrier(jnp.sum(grad_float * attn_rows.astype(jnp.float32), axis=1, keepdims=True))
            grad_scores = lax.optimization_barrier((weights * (grad_weights - row_delta)).astype(jnp.bfloat16)).astype(jnp.float32)
            grad_query = (jnp.einsum('qk,kd->qd', grad_scores, key_rows.astype(jnp.float32)) * scaling).astype(jnp.bfloat16)
            key_terms = jnp.einsum('qk,qd->kd', grad_scores, query_rows.astype(jnp.float32)) * scaling
            value_terms = jnp.einsum('qk,qd->kd', weights_bf, grad_float)
            all_terms = jnp.concatenate([key_terms, value_terms], axis=1).reshape(TOPK + 1, BLOCK, 2 * HD)
            return (grad_query, all_terms)
        grad_query, all_terms = jax.vmap(one_block)(query_blocks, key_sets, value_sets, usable, grad_blocks, attn_blocks)
        target_ids = jnp.concatenate([jnp.arange(NB, dtype=jnp.int32)[:, None], chosen_ids], axis=1)
        group_terms = all_terms.reshape(N_SEQ, QBD * (TOPK + 1), BLOCK, 2 * HD)
        group_targets = target_ids.reshape(N_SEQ, QBD * (TOPK + 1))

        def add_terms(carry, packed_group):
            group_id, targets_row, term_rows = packed_group
            group_sum = jnp.zeros((NB, BLOCK, 2 * HD), jnp.float32).at[targets_row].add(term_rows)
            rounded = lax.optimization_barrier(group_sum.astype(jnp.bfloat16)).astype(jnp.float32)
            keep_exact = (owner_of == group_id)[:, None, None]
            return (carry + jnp.where(keep_exact, group_sum, rounded), None)
        totals, _ = lax.scan(add_terms, jnp.zeros((NB, BLOCK, 2 * HD), jnp.float32), (jnp.arange(N_SEQ, dtype=jnp.int32), group_targets, group_terms))
        return (grad_query, totals[..., :HD].astype(jnp.bfloat16), totals[..., HD:].astype(jnp.bfloat16))
    grad_queries, grad_keys, grad_values = lax.map(backward_head, (jnp.arange(H, dtype=jnp.int32), attn_heads))

    def unblock(stacked):
        return stacked.transpose(1, 2, 0, 3).reshape(TOKENS, H * HD)
    return (projected, unblock(grad_queries), unblock(grad_keys), unblock(grad_values), weight_grad)
```

```python
import functools
import math

import jax
import jax.numpy as jnp
from jax import lax
from jax.experimental import pallas as pl
from jax.experimental.pallas import tpu as pltpu
from jax.sharding import PartitionSpec as P

ROW = 4
HEAD = 128
PIECE = 1024
EIGHTH = 2048
BLOCK = 512
ITEMS = 4
SLOTS = 5
ALL_BLOCKS = 32
MESH = pl.DeviceIdType.MESH
VMEM_LIMIT = 60 * 1024 * 1024
ANY = pl.BlockSpec(memory_space=pl.ANY)


def place():
    seq = lax.axis_index("seq")
    head = lax.axis_index("head")
    return seq // ROW, seq % ROW, head // 2, head % 2


def remote(src, dst, send_sem, recv_sem, device):
    return pltpu.make_async_remote_copy(
        src_ref=src,
        dst_ref=dst,
        send_sem=send_sem,
        recv_sem=recv_sem,
        device_id=device,
        device_id_type=MESH,
    )


def row_partner(k):
    y, x, z, c = place()
    device = (y * ROW + 2 * c + k, 2 * z + x // 2)
    return device, (x // 2 == c) & (x % 2 == k)


def signal_row_partners(barrier):
    for k in range(2):
        device, own = row_partner(k)

        @pl.when(jnp.logical_not(own))
        def _(device=device):
            pl.semaphore_signal(barrier, inc=1, device_id=device, device_id_type=MESH)


def row_partner_count():
    y, x, z, c = place()
    return 2 - (x // 2 == c).astype(jnp.int32)


def row_start(src, dst, send_sem, recv_sem, k):
    device, own = row_partner(k)

    @pl.when(jnp.logical_not(own))
    def _():
        remote(src, dst, send_sem, recv_sem, device).start()

    @pl.when(own)
    def _():
        pltpu.make_async_copy(src, dst, recv_sem).start()


def row_wait_recv(dst, recv_sem):
    pltpu.make_async_copy(dst, dst, recv_sem).wait()


def row_wait_send(src, dst, send_sem, recv_sem, k):
    device, own = row_partner(k)

    @pl.when(jnp.logical_not(own))
    def _():
        remote(src, dst, send_sem, recv_sem, device).wait_send()


def neighbours():
    y, x, z, c = place()
    up = (lax.rem(y + 1, ROW) * ROW + x, 2 * z + c)
    down = (lax.rem(y + ROW - 1, ROW) * ROW + x, 2 * z + c)
    sibling = (y * ROW + x, 2 * z + 1 - c)
    return up, down, sibling


def meet(with_ring):
    barrier = pltpu.get_barrier_semaphore()
    signal_row_partners(barrier)
    count = row_partner_count()
    if with_ring:
        for device in neighbours():
            pl.semaphore_signal(barrier, inc=1, device_id=device, device_id_type=MESH)
        count = count + 3
    pl.semaphore_wait(barrier, count)


def gather_kernel(
    q, k, v, do, sel, qn, kn, vn, don, seln,
    row_send, row_recv, ring_send, ring_recv, far_send, far_recv, sib_send, sib_recv,
):
    y, x, z, c = place()
    up, down, sibling = neighbours()
    meet(True)
    odd = x % 2
    home = pl.multiple_of((2 * y + x // 2) * EIGHTH + odd * PIECE, PIECE)
    spot = pl.multiple_of(odd * PIECE, PIECE)

    def row_refs(t, h):
        cols = pl.ds(h * HEAD, HEAD)
        if t == 0:
            return k.at[:, cols], kn.at[pl.ds(home, PIECE)]
        if t == 1:
            return v.at[:, cols], vn.at[pl.ds(home, PIECE)]
        if t == 2:
            return q.at[:, cols], qn.at[pl.ds(spot, PIECE)]
        if t == 3:
            return do.at[:, cols], don.at[pl.ds(spot, PIECE)]
        return sel.at[h], seln.at[odd]

    for t in range(5):
        for h in range(2):
            src, dst = row_refs(t, h)
            row_start(src, dst, row_send.at[t, h], row_recv.at[t, odd], h)

    kv = (kn, vn)

    def piece(t, shift, core, j):
        quarter = lax.rem(y + shift + ROW, ROW)
        start = pl.multiple_of((2 * quarter + core) * EIGHTH + j * PIECE, PIECE)
        return kv[t].at[pl.ds(start, PIECE)]

    def sib_copy(t, m, shift, j):
        own = piece(t, shift, c, j)
        return remote(own, own, sib_send.at[t, m, j], sib_recv.at[t, m, j], sibling)

    def ring_copy(t, way, j):
        own = piece(t, 0, c, j)
        return remote(
            own, own, ring_send.at[t, way, j], ring_recv.at[t, way, j], (up, down)[way]
        )

    def far_copy(t, way):
        own = piece(t, (-1, 1)[way], c, way)
        return remote(own, own, far_send.at[t, way], far_recv.at[t, way], (up, down)[way])

    for t in range(2):
        for j in range(2):
            row_wait_recv(piece(t, 0, c, j), row_recv.at[t, j])
            ring_copy(t, j, j).start()
            ring_copy(t, 1 - j, j).start()
            sib_copy(t, 0, 0, j).start()
    for t in range(2):
        for way in range(2):
            ring_copy(t, way, way).wait_recv()
            far_copy(t, way).start()
            sib_copy(t, 1 + way, (-1, 1)[way], way).start()
        for way in range(2):
            ring_copy(t, way, 1 - way).wait_recv()
            sib_copy(t, 1 + way, (-1, 1)[way], 1 - way).start()
    for t in range(2):
        for way in range(2):
            far_copy(t, way).wait_recv()
            sib_copy(t, 3, 2, way).start()
    for t in range(2, 5):
        for j in range(2):
            if t == 2:
                dst = qn.at[pl.ds(j * PIECE, PIECE)]
            elif t == 3:
                dst = don.at[pl.ds(j * PIECE, PIECE)]
            else:
                dst = seln.at[j]
            row_wait_recv(dst, row_recv.at[t, j])
    for t in range(5):
        for h in range(2):
            src, dst = row_refs(t, h)
            row_wait_send(src, dst, row_send.at[t, h], row_recv.at[t, odd], h)
    for t in range(2):
        for way in range(2):
            far_copy(t, way).wait_send()
            for j in range(2):
                ring_copy(t, way, j).wait_send()
        for m, shift in enumerate((0, -1, 1, 2)):
            for j in range(2):
                copy = sib_copy(t, m, shift, j)
                copy.wait_send()
                copy.wait_recv()


def gather(q, k, v, do, sel):
    half = jax.ShapeDtypeStruct((EIGHTH, HEAD), jnp.bfloat16)
    whole = jax.ShapeDtypeStruct((ALL_BLOCKS * BLOCK, HEAD), jnp.bfloat16)
    dma = pltpu.SemaphoreType.DMA
    return pl.pallas_call(
        gather_kernel,
        name="gather",
        out_shape=(half, whole, whole, half, jax.ShapeDtypeStruct((2, 8, 128), jnp.int32)),
        in_specs=[ANY] * 5,
        out_specs=(ANY,) * 5,
        scratch_shapes=[
            dma((5, 2)), dma((5, 2)), dma((2, 2, 2)), dma((2, 2, 2)),
            dma((2, 2)), dma((2, 2)), dma((2, 4, 2)), dma((2, 4, 2)),
        ],
        compiler_params=pltpu.CompilerParams(collective_id=0, has_side_effects=True),
        cost_estimate=pl.CostEstimate(flops=0, bytes_accessed=100_000_000, transcendentals=0),
    )(q, k, v, do, sel)


def dot(a, b, contract):
    return lax.dot_general(a, b, (contract, ((), ())), preferred_element_type=jnp.float32)


def attention_kernel(
    sel, q, do, k, v, out, dq, dk, dv, dk_sum, dv_sum, scores, expons
):
    y, x, z, c = place()
    scaling = 1.0 / math.sqrt(HEAD)
    factor = scaling * math.log2(math.e)

    @pl.loop(0, ALL_BLOCKS)
    def _(block):
        dk_sum[block] = jnp.zeros((BLOCK, HEAD), jnp.float32)
        dv_sum[block] = jnp.zeros((BLOCK, HEAD), jnp.float32)

    @pl.loop(0, ITEMS)
    def _(item):
        block = 8 * y + 4 * c + item
        rows = pl.ds(pl.multiple_of(item * BLOCK, BLOCK), BLOCK)
        query = q[rows, :]
        grad = do[rows, :]
        query_t = query.T
        grad_t = grad.T.astype(jnp.float32)
        ids = [block] + [sel[item // 2, item % 2, t] for t in range(SLOTS - 1)]
        top = jnp.full((1, BLOCK), -1e30, jnp.float32)
        for t in range(SLOTS):
            s = dot(k[ids[t]], query_t, ((1,), (0,)))
            if t == 0:
                key_at = lax.broadcasted_iota(jnp.int32, (BLOCK, BLOCK), 0)
                query_at = lax.broadcasted_iota(jnp.int32, (BLOCK, BLOCK), 1)
                s = jnp.where(key_at <= query_at, s, -1e30)
            else:
                s = jnp.where(ids[t] < block, s, -1e30)
            scores[t] = s
            top = jnp.maximum(top, jnp.max(s, axis=0, keepdims=True))
        top = top * factor
        total = jnp.zeros((1, BLOCK), jnp.float32)
        out_t = jnp.zeros((HEAD, BLOCK), jnp.float32)
        for t in range(SLOTS):
            e = jnp.exp2(scores[t] * factor - top)
            total = total + jnp.sum(e, axis=0, keepdims=True)
            eb = e.astype(jnp.bfloat16)
            expons[t] = eb
            out_t = out_t + dot(v[ids[t]], eb, ((0,), (0,)))
        inverse = 1.0 / total
        out_t = (out_t * inverse).astype(jnp.bfloat16)
        out[rows, :] = out_t.T
        delta = jnp.sum(grad_t * out_t.astype(jnp.float32), axis=0, keepdims=True) * inverse
        scaled_t = (grad_t * inverse).astype(jnp.bfloat16)
        scaled = scaled_t.T
        dq_t = jnp.zeros((HEAD, BLOCK), jnp.float32)
        for t in range(SLOTS):
            eb = expons[t]
            dp = dot(v[ids[t]], scaled_t, ((1,), (0,)))
            ds = (eb.astype(jnp.float32) * (dp - delta)).astype(jnp.bfloat16)
            dq_t = dq_t + dot(k[ids[t]], ds, ((0,), (0,)))
            dk_sum[ids[t]] += dot(ds, query, ((1,), (0,)))
            dv_sum[ids[t]] += dot(eb, scaled, ((1,), (0,)))
        dq[rows, :] = (dq_t * scaling).astype(jnp.bfloat16).T

    @pl.loop(0, ALL_BLOCKS)
    def _(block):
        dk[block] = (dk_sum[block] * scaling).astype(jnp.bfloat16)
        dv[block] = dv_sum[block].astype(jnp.bfloat16)


def attention(sel, q, do, k, v):
    half = jax.ShapeDtypeStruct((EIGHTH, HEAD), jnp.bfloat16)
    blocks = jax.ShapeDtypeStruct((ALL_BLOCKS, BLOCK, HEAD), jnp.bfloat16)
    vmem = pl.BlockSpec(memory_space=pltpu.VMEM)
    return pl.pallas_call(
        attention_kernel,
        name="attention",
        out_shape=(half, half, blocks, blocks),
        in_specs=[pl.BlockSpec(memory_space=pltpu.SMEM)] + [vmem] * 4,
        out_specs=(vmem,) * 4,
        scratch_shapes=[
            pltpu.VMEM((ALL_BLOCKS, BLOCK, HEAD), jnp.float32),
            pltpu.VMEM((ALL_BLOCKS, BLOCK, HEAD), jnp.float32),
            pltpu.VMEM((SLOTS, BLOCK, BLOCK), jnp.float32),
            pltpu.VMEM((SLOTS, BLOCK, BLOCK), jnp.bfloat16),
        ],
        compiler_params=pltpu.CompilerParams(vmem_limit_bytes=VMEM_LIMIT),
        cost_estimate=pl.CostEstimate(
            flops=8_000_000_000, bytes_accessed=20_000_000, transcendentals=5_000_000
        ),
    )(sel, q, do, k.reshape(ALL_BLOCKS, BLOCK, HEAD), v.reshape(ALL_BLOCKS, BLOCK, HEAD))


def back_refs(src, dst, j):
    y, x, z, c = place()
    cols = pl.ds(pl.multiple_of((x % 2) * HEAD, HEAD), HEAD)
    return src.at[pl.ds(j * PIECE, PIECE)], dst.at[:, cols]


def return_kernel(out, attn, send, recv):
    y, x, z, c = place()
    odd = x % 2
    meet(False)
    for j in range(2):
        src, dst = back_refs(out, attn, j)
        row_start(src, dst, send.at[j], recv.at[odd], j)
    for h in range(2):
        row_wait_recv(attn.at[:, pl.ds(h * HEAD, HEAD)], recv.at[h])
    for j in range(2):
        src, dst = back_refs(out, attn, j)
        row_wait_send(src, dst, send.at[j], recv.at[odd], j)


def return_attention(out):
    return pl.pallas_call(
        return_kernel,
        name="return_attention",
        out_shape=jax.ShapeDtypeStruct((PIECE, 2 * HEAD), jnp.bfloat16),
        in_specs=[ANY],
        out_specs=ANY,
        scratch_shapes=[pltpu.SemaphoreType.DMA((2,)), pltpu.SemaphoreType.DMA((2,))],
        compiler_params=pltpu.CompilerParams(collective_id=1, has_side_effects=True),
        cost_estimate=pl.CostEstimate(flops=0, bytes_accessed=20_000_000, transcendentals=0),
    )(out)


SHIFTS = (0, -1, 1, 2)
STEP = 256


def reduce_kernel(
    dq, dk, dv, dq_home, dk_home, dv_home, mine, theirs, near, far,
    row_send, row_recv, load, sib_send, sib_recv, ring_send, ring_recv, far_send, far_recv,
):
    y, x, z, c = place()
    up, down, sibling = neighbours()
    odd = x % 2
    meet(True)
    parts = (dk, dv)
    homes = (dk_home, dv_home)

    def eighth(t, shift, core):
        quarter = lax.rem(y + shift + ROW, ROW)
        start = pl.multiple_of((2 * quarter + core) * EIGHTH, EIGHTH)
        return parts[t].at[pl.ds(start, EIGHTH)]

    def load_copy(t, m):
        return pltpu.make_async_copy(eighth(t, SHIFTS[m], c), mine.at[t, m], load.at[t, m])

    def sib_copy(t, m):
        return remote(
            eighth(t, SHIFTS[m], 1 - c), theirs.at[t, m],
            sib_send.at[t, m], sib_recv.at[t, m], sibling,
        )

    def half(ref, j):
        return ref.at[pl.ds(j * PIECE, PIECE)]

    def far_copy(t, way):
        return remote(
            half(mine.at[t, 3], way), far.at[t, way],
            far_send.at[t, way], far_recv.at[t, way], (up, down)[way],
        )

    def ring_copy(t, way, j):
        return remote(
            half(mine.at[t, 2 - way], j), near.at[t, way, j],
            ring_send.at[t, way, j], ring_recv.at[t, way, j], (up, down)[way],
        )

    def add_theirs(t, m):
        load_copy(t, m).wait()
        sib_copy(t, m).wait_recv()

        @pl.loop(0, EIGHTH // STEP)
        def _(i):
            rows = pl.ds(pl.multiple_of(i * STEP, STEP), STEP)
            total = mine[t, m, rows, :].astype(jnp.float32)
            total = total + theirs[t, m, rows, :].astype(jnp.float32)
            mine[t, m, rows, :] = total.astype(jnp.bfloat16)

    for m in (3, 1, 2, 0):
        for t in range(2):
            sib_copy(t, m).start()
            load_copy(t, m).start()
    for j in range(2):
        src, dst = back_refs(dq, dq_home, j)
        row_start(src, dst, row_send.at[2, j], row_recv.at[2, odd], j)

    for t in range(2):
        add_theirs(t, 3)
        for way in range(2):
            far_copy(t, way).start()
    for t in range(2):
        for way in range(2):
            add_theirs(t, 2 - way)
            ring_copy(t, way, 1 - way).start()
    for t in range(2):
        for way in range(2):
            far_copy(t, way).wait_recv()

            @pl.loop(0, PIECE // STEP)
            def _(i, t=t, way=way):
                there = pl.ds(pl.multiple_of(i * STEP, STEP), STEP)
                here = pl.ds(pl.multiple_of(way * PIECE + i * STEP, STEP), STEP)
                total = mine[t, 2 - way, here, :].astype(jnp.float32)
                total = total + far[t, way, there, :].astype(jnp.float32)
                mine[t, 2 - way, here, :] = total.astype(jnp.bfloat16)

            ring_copy(t, way, way).start()
    for t in range(2):
        load_copy(t, 0).wait()
        sib_copy(t, 0).wait_recv()
        for j in range(2):
            for way in range(2):
                ring_copy(t, way, j).wait_recv()

            @pl.loop(0, PIECE // STEP)
            def _(i, t=t, j=j):
                there = pl.ds(pl.multiple_of(i * STEP, STEP), STEP)
                here = pl.ds(pl.multiple_of(j * PIECE + i * STEP, STEP), STEP)
                total = mine[t, 0, here, :].astype(jnp.float32)
                total = total + theirs[t, 0, here, :].astype(jnp.float32)
                total = total + near[t, 0, j, there, :].astype(jnp.float32)
                total = total + near[t, 1, j, there, :].astype(jnp.float32)
                mine[t, 0, here, :] = total.astype(jnp.bfloat16)

            src, dst = back_refs(mine.at[t, 0], homes[t], j)
            row_start(src, dst, row_send.at[t, j], row_recv.at[t, odd], j)

    all_homes = homes + (dq_home,)
    for t in range(3):
        for h in range(2):
            row_wait_recv(all_homes[t].at[:, pl.ds(h * HEAD, HEAD)], row_recv.at[t, h])
        for j in range(2):
            src, dst = back_refs(mine.at[t, 0] if t < 2 else dq, all_homes[t], j)
            row_wait_send(src, dst, row_send.at[t, j], row_recv.at[t, odd], j)
    for t in range(2):
        for m in range(4):
            sib_copy(t, m).wait_send()
        for way in range(2):
            far_copy(t, way).wait_send()
            for j in range(2):
                ring_copy(t, way, j).wait_send()


def reduce_home(dq, dk, dv):
    home = jax.ShapeDtypeStruct((PIECE, 2 * HEAD), jnp.bfloat16)
    dma = pltpu.SemaphoreType.DMA
    return pl.pallas_call(
        reduce_kernel,
        name="reduce_home",
        out_shape=(home,) * 3,
        in_specs=[ANY] * 3,
        out_specs=(ANY,) * 3,
        scratch_shapes=[
            pltpu.VMEM((2, 4, EIGHTH, HEAD), jnp.bfloat16),
            pltpu.VMEM((2, 4, EIGHTH, HEAD), jnp.bfloat16),
            pltpu.VMEM((2, 2, 2, PIECE, HEAD), jnp.bfloat16),
            pltpu.VMEM((2, 2, PIECE, HEAD), jnp.bfloat16),
            dma((3, 2)), dma((3, 2)), dma((2, 4)), dma((2, 4)), dma((2, 4)),
            dma((2, 2, 2)), dma((2, 2, 2)), dma((2, 2)), dma((2, 2)),
        ],
        compiler_params=pltpu.CompilerParams(
            collective_id=2, has_side_effects=True, vmem_limit_bytes=VMEM_LIMIT
        ),
        cost_estimate=pl.CostEstimate(flops=0, bytes_accessed=150_000_000, transcendentals=0),
    )(dq, dk.reshape(-1, HEAD), dv.reshape(-1, HEAD))


def shards(queries, key_states, values, selection, out_weight, cotangent):
    grad_attn = dot(cotangent, out_weight, ((1,), (1,))).astype(jnp.bfloat16)
    sel = jnp.pad(selection, ((0, 0), (0, 6), (0, 124)))
    q, k, v, do, sel = gather(queries, key_states, values, grad_attn, sel)
    out, dq, dk, dv = attention(sel, q, do, k, v)
    attn = return_attention(out)
    part = dot(attn, out_weight, ((1,), (0,))).astype(jnp.bfloat16)
    weight_part = dot(attn, cotangent, ((0,), (0,))).astype(jnp.bfloat16)
    part, weight_part, dq = lax.optimization_barrier((part, weight_part, dq))
    projected = lax.psum_scatter(part, "head", scatter_dimension=0, tiled=True)
    weight_grad = lax.psum_scatter(weight_part, "seq", scatter_dimension=1, tiled=True)
    query_grad, key_grad, value_grad = reduce_home(dq, dk, dv)
    return projected, query_grad, key_grad, value_grad, weight_grad.astype(jnp.float32)


def solution(mesh):
    in_specs = (
        P("seq", "head"),
        P("seq", "head"),
        P("seq", "head"),
        P("head", "seq", None),
        P("head", None),
        P("seq", None),
    )
    out_specs = (
        P(("seq", "head"), None),
        P("seq", "head"),
        P("seq", "head"),
        P("seq", "head"),
        P("head", "seq"),
    )
    return jax.shard_map(shards, mesh=mesh, in_specs=in_specs, out_specs=out_specs, check_vma=False)
```

```python
import functools
import math

import jax
import jax.numpy as jnp
from jax import lax
from jax.experimental import pallas as pl
from jax.experimental.pallas import tpu as pltpu
from jax.sharding import PartitionSpec as P

ROW = 4
HEAD = 128
PIECE = 1024
EIGHTH = 2048
BLOCK = 512
ITEMS = 4
SLOTS = 5
ALL_BLOCKS = 32
MESH = pl.DeviceIdType.MESH
VMEM_LIMIT = 60 * 1024 * 1024
ANY = pl.BlockSpec(memory_space=pl.ANY)


def place():
    seq = lax.axis_index("seq")
    head = lax.axis_index("head")
    return seq // ROW, seq % ROW, head // 2, head % 2


def remote(src, dst, send_sem, recv_sem, device):
    return pltpu.make_async_remote_copy(
        src_ref=src,
        dst_ref=dst,
        send_sem=send_sem,
        recv_sem=recv_sem,
        device_id=device,
        device_id_type=MESH,
    )


def row_partner(k):
    y, x, z, c = place()
    device = (y * ROW + 2 * c + k, 2 * z + x // 2)
    return device, (x // 2 == c) & (x % 2 == k)


def signal_row_partners(barrier):
    for k in range(2):
        device, own = row_partner(k)

        @pl.when(jnp.logical_not(own))
        def _(device=device):
            pl.semaphore_signal(barrier, inc=1, device_id=device, device_id_type=MESH)


def row_partner_count():
    y, x, z, c = place()
    return 2 - (x // 2 == c).astype(jnp.int32)


def row_start(src, dst, send_sem, recv_sem, k):
    device, own = row_partner(k)

    @pl.when(jnp.logical_not(own))
    def _():
        remote(src, dst, send_sem, recv_sem, device).start()

    @pl.when(own)
    def _():
        pltpu.make_async_copy(src, dst, recv_sem).start()


def row_wait_recv(dst, recv_sem):
    pltpu.make_async_copy(dst, dst, recv_sem).wait()


def row_wait_send(src, dst, send_sem, recv_sem, k):
    device, own = row_partner(k)

    @pl.when(jnp.logical_not(own))
    def _():
        remote(src, dst, send_sem, recv_sem, device).wait_send()


def neighbours():
    y, x, z, c = place()
    up = (lax.rem(y + 1, ROW) * ROW + x, 2 * z + c)
    down = (lax.rem(y + ROW - 1, ROW) * ROW + x, 2 * z + c)
    sibling = (y * ROW + x, 2 * z + 1 - c)
    return up, down, sibling


def meet(others):
    barrier = pltpu.get_barrier_semaphore()
    signal_row_partners(barrier)
    for device in others:
        pl.semaphore_signal(barrier, inc=1, device_id=device, device_id_type=MESH)
    pl.semaphore_wait(barrier, row_partner_count() + len(others))


def gather_kernel(
    q, k, v, do, sel, qn, kn, vn, don, seln,
    row_send, row_recv, ring_send, ring_recv, far_send, far_recv, sib_send, sib_recv,
):
    y, x, z, c = place()
    up, down, sibling = neighbours()
    meet(neighbours())
    odd = x % 2
    home = pl.multiple_of((2 * y + x // 2) * EIGHTH + odd * PIECE, PIECE)
    spot = pl.multiple_of(odd * PIECE, PIECE)

    def row_refs(t, h):
        cols = pl.ds(h * HEAD, HEAD)
        if t == 0:
            return k.at[:, cols], kn.at[pl.ds(home, PIECE)]
        if t == 1:
            return v.at[:, cols], vn.at[pl.ds(home, PIECE)]
        if t == 2:
            return q.at[:, cols], qn.at[pl.ds(spot, PIECE)]
        if t == 3:
            return do.at[:, cols], don.at[pl.ds(spot, PIECE)]
        return sel.at[h], seln.at[odd]

    for t in range(5):
        for h in range(2):
            src, dst = row_refs(t, h)
            row_start(src, dst, row_send.at[t, h], row_recv.at[t, odd], h)

    kv = (kn, vn)

    def piece(t, shift, core, j):
        quarter = lax.rem(y + shift + ROW, ROW)
        start = pl.multiple_of((2 * quarter + core) * EIGHTH + j * PIECE, PIECE)
        return kv[t].at[pl.ds(start, PIECE)]

    def sib_copy(t, m, shift, j):
        own = piece(t, shift, c, j)
        return remote(own, own, sib_send.at[t, m, j], sib_recv.at[t, m, j], sibling)

    def ring_copy(t, way, j):
        own = piece(t, 0, c, j)
        return remote(
            own, own, ring_send.at[t, way, j], ring_recv.at[t, way, j], (up, down)[way]
        )

    def far_copy(t, way):
        own = piece(t, (-1, 1)[way], c, way)
        return remote(own, own, far_send.at[t, way], far_recv.at[t, way], (up, down)[way])

    for t in range(2):
        for j in range(2):
            row_wait_recv(piece(t, 0, c, j), row_recv.at[t, j])
            ring_copy(t, j, j).start()
            ring_copy(t, 1 - j, j).start()
            sib_copy(t, 0, 0, j).start()
    for t in range(2):
        for way in range(2):
            ring_copy(t, way, way).wait_recv()
            far_copy(t, way).start()
            sib_copy(t, 1 + way, (-1, 1)[way], way).start()
        for way in range(2):
            ring_copy(t, way, 1 - way).wait_recv()
            sib_copy(t, 1 + way, (-1, 1)[way], 1 - way).start()
    for t in range(2):
        for way in range(2):
            far_copy(t, way).wait_recv()
            sib_copy(t, 3, 2, way).start()
    for t in range(2, 5):
        for j in range(2):
            if t == 2:
                dst = qn.at[pl.ds(j * PIECE, PIECE)]
            elif t == 3:
                dst = don.at[pl.ds(j * PIECE, PIECE)]
            else:
                dst = seln.at[j]
            row_wait_recv(dst, row_recv.at[t, j])
    for t in range(5):
        for h in range(2):
            src, dst = row_refs(t, h)
            row_wait_send(src, dst, row_send.at[t, h], row_recv.at[t, odd], h)
    for t in range(2):
        for way in range(2):
            far_copy(t, way).wait_send()
            for j in range(2):
                ring_copy(t, way, j).wait_send()
        for m, shift in enumerate((0, -1, 1, 2)):
            for j in range(2):
                copy = sib_copy(t, m, shift, j)
                copy.wait_send()
                copy.wait_recv()


def gather(q, k, v, do, sel):
    half = jax.ShapeDtypeStruct((EIGHTH, HEAD), jnp.bfloat16)
    whole = jax.ShapeDtypeStruct((ALL_BLOCKS * BLOCK, HEAD), jnp.bfloat16)
    dma = pltpu.SemaphoreType.DMA
    return pl.pallas_call(
        gather_kernel,
        name="gather",
        out_shape=(half, whole, whole, half, jax.ShapeDtypeStruct((2, 8, 128), jnp.int32)),
        in_specs=[ANY] * 5,
        out_specs=(ANY,) * 5,
        scratch_shapes=[
            dma((5, 2)), dma((5, 2)), dma((2, 2, 2)), dma((2, 2, 2)),
            dma((2, 2)), dma((2, 2)), dma((2, 4, 2)), dma((2, 4, 2)),
        ],
        compiler_params=pltpu.CompilerParams(collective_id=0, has_side_effects=True),
        cost_estimate=pl.CostEstimate(flops=0, bytes_accessed=100_000_000, transcendentals=0),
    )(q, k, v, do, sel)


def dot(a, b, contract):
    return lax.dot_general(a, b, (contract, ((), ())), preferred_element_type=jnp.float32)


def attention_kernel(
    sel, q, do, k, v, out, dq, dk, dv, dk_sum, dv_sum, scores, expons
):
    y, x, z, c = place()
    scaling = 1.0 / math.sqrt(HEAD)
    factor = scaling * math.log2(math.e)

    @pl.loop(0, ALL_BLOCKS)
    def _(block):
        dk_sum[block] = jnp.zeros((BLOCK, HEAD), jnp.float32)
        dv_sum[block] = jnp.zeros((BLOCK, HEAD), jnp.float32)

    @pl.loop(0, ITEMS)
    def _(item):
        block = 8 * y + 4 * c + item
        rows = pl.ds(pl.multiple_of(item * BLOCK, BLOCK), BLOCK)
        query = q[rows, :]
        grad = do[rows, :]
        query_t = query.T
        grad_t = grad.T.astype(jnp.float32)
        ids = [block] + [sel[item // 2, item % 2, t] for t in range(SLOTS - 1)]
        top = jnp.full((1, BLOCK), -1e30, jnp.float32)
        for t in range(SLOTS):
            s = dot(k[ids[t]], query_t, ((1,), (0,)))
            if t == 0:
                key_at = lax.broadcasted_iota(jnp.int32, (BLOCK, BLOCK), 0)
                query_at = lax.broadcasted_iota(jnp.int32, (BLOCK, BLOCK), 1)
                s = jnp.where(key_at <= query_at, s, -1e30)
            else:
                s = jnp.where(ids[t] < block, s, -1e30)
            scores[t] = s
            top = jnp.maximum(top, jnp.max(s, axis=0, keepdims=True))
        top = top * factor
        total = jnp.zeros((1, BLOCK), jnp.float32)
        out_t = jnp.zeros((HEAD, BLOCK), jnp.float32)
        for t in range(SLOTS):
            e = jnp.exp2(scores[t] * factor - top)
            total = total + jnp.sum(e, axis=0, keepdims=True)
            eb = e.astype(jnp.bfloat16)
            expons[t] = eb
            out_t = out_t + dot(v[ids[t]], eb, ((0,), (0,)))
        inverse = 1.0 / total
        out_t = (out_t * inverse).astype(jnp.bfloat16)
        out[rows, :] = out_t.T
        delta = jnp.sum(grad_t * out_t.astype(jnp.float32), axis=0, keepdims=True) * inverse
        scaled_t = (grad_t * inverse).astype(jnp.bfloat16)
        scaled = scaled_t.T
        dq_t = jnp.zeros((HEAD, BLOCK), jnp.float32)
        for t in range(SLOTS):
            eb = expons[t]
            dp = dot(v[ids[t]], scaled_t, ((1,), (0,)))
            ds = (eb.astype(jnp.float32) * (dp - delta)).astype(jnp.bfloat16)
            dq_t = dq_t + dot(k[ids[t]], ds, ((0,), (0,)))
            dk_sum[ids[t]] += dot(ds, query, ((1,), (0,)))
            dv_sum[ids[t]] += dot(eb, scaled, ((1,), (0,)))
        dq[rows, :] = (dq_t * scaling).astype(jnp.bfloat16).T

    @pl.loop(0, ALL_BLOCKS)
    def _(block):
        dk[block] = (dk_sum[block] * scaling).astype(jnp.bfloat16)
        dv[block] = dv_sum[block].astype(jnp.bfloat16)


def attention(sel, q, do, k, v):
    half = jax.ShapeDtypeStruct((EIGHTH, HEAD), jnp.bfloat16)
    blocks = jax.ShapeDtypeStruct((ALL_BLOCKS, BLOCK, HEAD), jnp.bfloat16)
    vmem = pl.BlockSpec(memory_space=pltpu.VMEM)
    return pl.pallas_call(
        attention_kernel,
        name="attention",
        out_shape=(half, half, blocks, blocks),
        in_specs=[pl.BlockSpec(memory_space=pltpu.SMEM)] + [vmem] * 4,
        out_specs=(vmem,) * 4,
        scratch_shapes=[
            pltpu.VMEM((ALL_BLOCKS, BLOCK, HEAD), jnp.float32),
            pltpu.VMEM((ALL_BLOCKS, BLOCK, HEAD), jnp.float32),
            pltpu.VMEM((SLOTS, BLOCK, BLOCK), jnp.float32),
            pltpu.VMEM((SLOTS, BLOCK, BLOCK), jnp.bfloat16),
        ],
        compiler_params=pltpu.CompilerParams(vmem_limit_bytes=VMEM_LIMIT),
        cost_estimate=pl.CostEstimate(
            flops=8_000_000_000, bytes_accessed=20_000_000, transcendentals=5_000_000
        ),
    )(sel, q, do, k.reshape(ALL_BLOCKS, BLOCK, HEAD), v.reshape(ALL_BLOCKS, BLOCK, HEAD))


def back_refs(src, dst, j):
    y, x, z, c = place()
    cols = pl.ds(pl.multiple_of((x % 2) * HEAD, HEAD), HEAD)
    return src.at[pl.ds(j * PIECE, PIECE)], dst.at[:, cols]


SHIFTS = (0, -1, 1, 2)
STEP = 256
DEPTH = 8
CHUNK = 64


def reduce_kernel(
    out, dq, dk, dv, weight, cotangent,
    projected, dq_home, dk_home, dv_home, weight_grad,
    attn, mine, theirs, near, far, part, part_sib, part_in, chunks, chunk_sum, row_in, col_in,
    row_send, row_recv, load, sib_send, sib_recv, ring_send, ring_recv, far_send, far_recv,
    part_send, part_recv, z_send, z_recv, wx_send, wx_recv, wy_send, wy_recv,
):
    y, x, z, c = place()
    up, down, sibling = neighbours()
    odd = x % 2
    z_next = (y * ROW + x, 2 * lax.rem(z + 1, DEPTH) + c)
    z_last = (y * ROW + x, 2 * lax.rem(z + DEPTH - 1, DEPTH) + c)
    across = [(y * ROW + lax.rem(x + d, ROW), 2 * z + c) for d in range(1, ROW)]
    along = [(lax.rem(y + d, ROW) * ROW + x, 2 * z + c) for d in range(1, ROW)]
    meet([up, down, sibling, z_next, z_last, along[1]] + across)
    parts = (dk, dv)
    homes = (dk_home, dv_home, dq_home, attn)
    sources = (mine.at[0, 0], mine.at[1, 0], dq, out)

    def go_home(t, j):
        src, dst = back_refs(sources[t], homes[t], j)
        row_start(src, dst, row_send.at[t, j], row_recv.at[t, odd], j)

    def eighth(t, shift, core):
        quarter = lax.rem(y + shift + ROW, ROW)
        start = pl.multiple_of((2 * quarter + core) * EIGHTH, EIGHTH)
        return parts[t].at[pl.ds(start, EIGHTH)]

    def load_copy(t, m):
        return pltpu.make_async_copy(eighth(t, SHIFTS[m], c), mine.at[t, m], load.at[t, m])

    def sib_copy(t, m):
        return remote(
            eighth(t, SHIFTS[m], 1 - c), theirs.at[t, m],
            sib_send.at[t, m], sib_recv.at[t, m], sibling,
        )

    def half(ref, j):
        return ref.at[pl.ds(j * PIECE, PIECE)]

    def far_copy(t, way):
        return remote(
            half(mine.at[t, 3], way), far.at[t, way],
            far_send.at[t, way], far_recv.at[t, way], (up, down)[way],
        )

    def ring_copy(t, way, j):
        return remote(
            half(mine.at[t, 2 - way], j), near.at[t, way, j],
            ring_send.at[t, way, j], ring_recv.at[t, way, j], (up, down)[way],
        )

    def add_theirs(t, m):
        load_copy(t, m).wait()
        sib_copy(t, m).wait_recv()

        @pl.loop(0, EIGHTH // STEP)
        def _(i):
            rows = pl.ds(pl.multiple_of(i * STEP, STEP), STEP)
            total = mine[t, m, rows, :].astype(jnp.float32)
            total = total + theirs[t, m, rows, :].astype(jnp.float32)
            mine[t, m, rows, :] = total.astype(jnp.bfloat16)

    def add_far(t, way):
        far_copy(t, way).wait_recv()

        @pl.loop(0, PIECE // STEP)
        def _(i):
            there = pl.ds(pl.multiple_of(i * STEP, STEP), STEP)
            here = pl.ds(pl.multiple_of(way * PIECE + i * STEP, STEP), STEP)
            total = mine[t, 2 - way, here, :].astype(jnp.float32)
            total = total + far[t, way, there, :].astype(jnp.float32)
            mine[t, 2 - way, here, :] = total.astype(jnp.bfloat16)

        ring_copy(t, way, way).start()

    def finish(t, j):
        for way in range(2):
            ring_copy(t, way, j).wait_recv()

        @pl.loop(0, PIECE // STEP)
        def _(i):
            there = pl.ds(pl.multiple_of(i * STEP, STEP), STEP)
            here = pl.ds(pl.multiple_of(j * PIECE + i * STEP, STEP), STEP)
            total = mine[t, 0, here, :].astype(jnp.float32)
            total = total + theirs[t, 0, here, :].astype(jnp.float32)
            total = total + near[t, 0, j, there, :].astype(jnp.float32)
            total = total + near[t, 1, j, there, :].astype(jnp.float32)
            mine[t, 0, here, :] = total.astype(jnp.bfloat16)

        go_home(t, j)

    def part_copy():
        return remote(part.at[:, 1 - c], part_sib, part_send, part_recv, sibling)

    def z_at(shift):
        return lax.rem(z + shift + DEPTH, DEPTH)

    def z_copy(way, step):
        src = part.at[z_at(step if way == 0 else -step), c]
        dst = part_in.at[way, step - 1]
        if step == DEPTH // 2:
            rows = pl.ds(way * (CHUNK // 2), CHUNK // 2)
            src, dst = src.at[rows], dst.at[rows]
        return remote(
            src, dst, z_send.at[way, step - 1], z_recv.at[way, step - 1], (z_next, z_last)[way]
        )

    def z_step(step):
        for way in range(2):
            z_copy(way, step + 1).wait_recv()
            mine_at = z_at(step if way == 0 else -step)
            rows = pl.ds(0, CHUNK)
            if step + 1 == DEPTH // 2:
                rows = pl.ds(way * (CHUNK // 2), CHUNK // 2)
            total = part[mine_at, c, rows, :].astype(jnp.float32)
            total = total + part_in[way, step, rows, :].astype(jnp.float32)
            part[mine_at, c, rows, :] = total.astype(jnp.bfloat16)
            z_copy(way, step).start()

    def project():
        @pl.loop(0, 4)
        def _(i):
            rows = pl.ds(pl.multiple_of(i * 256, 256), 256)
            for n in range(4):
                cols = pl.ds(n * 512, 512)
                tile = dot(attn[rows, :], weight[:, cols], ((1,), (0,))).astype(jnp.bfloat16)
                for a in range(2):
                    for b in range(2):
                        at = (2 * a + b) * CHUNK
                        part[2 * i + a, b, :, cols] = tile[at : at + CHUNK, :]

        part_copy().start()

    def project_sum():
        part_copy().wait()

        @pl.loop(0, DEPTH)
        def _(i):
            total = part[i, c].astype(jnp.float32) + part_sib[i].astype(jnp.float32)
            part[i, c] = total.astype(jnp.bfloat16)

        for way in range(2):
            z_copy(way, DEPTH // 2).start()

    def project_end():
        total = part[z, c].astype(jnp.float32)
        for way in range(2):
            z_copy(way, 1).wait_recv()
            total = total + part_in[way, 0].astype(jnp.float32)
        projected[...] = total.astype(jnp.bfloat16)

    def across_copy(d):
        return remote(
            chunks.at[lax.rem(x + d, ROW)], row_in.at[d - 1],
            wx_send.at[d - 1], wx_recv.at[d - 1], across[d - 1],
        )

    def along_copy(d):
        return remote(
            chunk_sum.at[lax.rem(y + d, ROW)], col_in.at[d - 1],
            wy_send.at[d - 1], wy_recv.at[d - 1], along[d - 1],
        )

    def weight_start():
        attn_t = attn[...].T
        for yy in range(ROW):
            tile = dot(attn_t, cotangent[:, yy * 512 : (yy + 1) * 512], ((1,), (0,)))
            for xx in range(ROW):
                chunks[xx, yy] = tile[:, xx * 128 : (xx + 1) * 128].astype(jnp.bfloat16)
        for d in range(1, ROW):
            across_copy(d).start()

    def weight_middle():
        for d in range(1, ROW):
            across_copy(d).wait_recv()
        for yy in range(ROW):
            total = chunks[x, yy].astype(jnp.float32)
            for d in range(ROW - 1):
                total = total + row_in[d, yy].astype(jnp.float32)
            chunk_sum[yy] = total.astype(jnp.bfloat16)
        for d in range(1, ROW):
            along_copy(d).start()

    def weight_end():
        total = chunk_sum[y].astype(jnp.float32)
        for d in range(1, ROW):
            along_copy(d).wait_recv()
            total = total + col_in[d - 1].astype(jnp.float32)
        weight_grad[...] = total

    for j in range(2):
        go_home(3, j)
    for m in (3, 1, 2, 0):
        for t in range(2):
            sib_copy(t, m).start()
            load_copy(t, m).start()
    for j in range(2):
        go_home(2, j)

    for t in range(2):
        add_theirs(t, 3)
        for way in range(2):
            far_copy(t, way).start()
    for h in range(2):
        row_wait_recv(attn.at[:, pl.ds(h * HEAD, HEAD)], row_recv.at[3, h])
    project()
    for t in range(2):
        for way in range(2):
            add_theirs(t, 2 - way)
            ring_copy(t, way, 1 - way).start()
    project_sum()
    weight_start()
    for way in range(2):
        add_far(0, way)
    z_step(3)
    for way in range(2):
        add_far(1, way)
    weight_middle()
    z_step(2)
    for t in range(2):
        load_copy(t, 0).wait()
        sib_copy(t, 0).wait_recv()
    finish(0, 0)
    z_step(1)
    finish(0, 1)
    project_end()
    weight_end()
    finish(1, 0)
    finish(1, 1)

    for t in range(4):
        if t < 3:
            for h in range(2):
                row_wait_recv(homes[t].at[:, pl.ds(h * HEAD, HEAD)], row_recv.at[t, h])
        for j in range(2):
            src, dst = back_refs(sources[t], homes[t], j)
            row_wait_send(src, dst, row_send.at[t, j], row_recv.at[t, odd], j)
    for t in range(2):
        for m in range(4):
            sib_copy(t, m).wait_send()
        for way in range(2):
            far_copy(t, way).wait_send()
            for j in range(2):
                ring_copy(t, way, j).wait_send()
    for step in range(1, DEPTH // 2 + 1):
        for way in range(2):
            z_copy(way, step).wait_send()
    for d in range(1, ROW):
        across_copy(d).wait_send()
        along_copy(d).wait_send()


def reduce_home(out, dq, dk, dv, weight, cotangent):
    home = jax.ShapeDtypeStruct((PIECE, 2 * HEAD), jnp.bfloat16)
    dma = pltpu.SemaphoreType.DMA
    vmem = pl.BlockSpec(memory_space=pltpu.VMEM)
    wide = weight.shape[1]
    bf16 = jnp.bfloat16
    return pl.pallas_call(
        reduce_kernel,
        name="reduce_home",
        out_shape=(
            jax.ShapeDtypeStruct((CHUNK, wide), bf16),
            home, home, home,
            jax.ShapeDtypeStruct((2 * HEAD, HEAD), jnp.float32),
        ),
        in_specs=[ANY] * 4 + [vmem] * 2,
        out_specs=(vmem, ANY, ANY, ANY, vmem),
        scratch_shapes=[
            pltpu.VMEM((PIECE, 2 * HEAD), bf16),
            pltpu.VMEM((2, 4, EIGHTH, HEAD), bf16),
            pltpu.VMEM((2, 4, EIGHTH, HEAD), bf16),
            pltpu.VMEM((2, 2, 2, PIECE, HEAD), bf16),
            pltpu.VMEM((2, 2, PIECE, HEAD), bf16),
            pltpu.VMEM((DEPTH, 2, CHUNK, wide), bf16),
            pltpu.VMEM((DEPTH, CHUNK, wide), bf16),
            pltpu.VMEM((2, DEPTH // 2, CHUNK, wide), bf16),
            pltpu.VMEM((ROW, ROW, 2 * HEAD, HEAD), bf16),
            pltpu.VMEM((ROW, 2 * HEAD, HEAD), bf16),
            pltpu.VMEM((ROW - 1, ROW, 2 * HEAD, HEAD), bf16),
            pltpu.VMEM((ROW - 1, 2 * HEAD, HEAD), bf16),
            dma((4, 2)), dma((4, 2)), dma((2, 4)), dma((2, 4)), dma((2, 4)),
            dma((2, 2, 2)), dma((2, 2, 2)), dma((2, 2)), dma((2, 2)),
            dma, dma, dma((2, 4)), dma((2, 4)), dma((3,)), dma((3,)), dma((3,)), dma((3,)),
        ],
        compiler_params=pltpu.CompilerParams(
            collective_id=2, has_side_effects=True, vmem_limit_bytes=VMEM_LIMIT
        ),
        cost_estimate=pl.CostEstimate(flops=0, bytes_accessed=150_000_000, transcendentals=0),
    )(out, dq, dk.reshape(-1, HEAD), dv.reshape(-1, HEAD), weight, cotangent)


def settle_kernel(*refs):
    sems = refs[-1]
    count = (len(refs) - 1) // 2
    copies = [
        pltpu.make_async_copy(refs[i], refs[count + i], sems.at[i]) for i in range(count)
    ]
    for copy in copies:
        copy.start()
    for copy in copies:
        copy.wait()


def settle(*arrays):
    return pl.pallas_call(
        settle_kernel,
        name="settle",
        out_shape=tuple(jax.ShapeDtypeStruct(a.shape, a.dtype) for a in arrays),
        in_specs=[ANY] * len(arrays),
        out_specs=(ANY,) * len(arrays),
        scratch_shapes=[pltpu.SemaphoreType.DMA((len(arrays),))],
    )(*arrays)


def shards(queries, key_states, values, selection, out_weight, cotangent):
    grad_attn = dot(cotangent, out_weight, ((1,), (1,))).astype(jnp.bfloat16)
    sel = jnp.pad(selection, ((0, 0), (0, 6), (0, 124)))
    q, k, v, do, sel = gather(queries, key_states, values, grad_attn, sel)
    out, dq, dk, dv = attention(sel, q, do, k, v)
    return settle(*reduce_home(out, dq, dk, dv, out_weight, cotangent))


def solution(mesh):
    in_specs = (
        P("seq", "head"),
        P("seq", "head"),
        P("seq", "head"),
        P("head", "seq", None),
        P("head", None),
        P("seq", None),
    )
    out_specs = (
        P(("seq", "head"), None),
        P("seq", "head"),
        P("seq", "head"),
        P("seq", "head"),
        P("head", "seq"),
    )
    return jax.shard_map(shards, mesh=mesh, in_specs=in_specs, out_specs=out_specs, check_vma=False)
```

```python
import functools
import math

import jax
import jax.numpy as jnp
from jax import lax
from jax.experimental import pallas as pl
from jax.experimental.pallas import tpu as pltpu
from jax.sharding import PartitionSpec as P

ROW = 4
HEAD = 128
PIECE = 1024
EIGHTH = 2048
BLOCK = 512
ITEMS = 4
SLOTS = 5
ALL_BLOCKS = 32
MESH = pl.DeviceIdType.MESH
VMEM_LIMIT = 60 * 1024 * 1024
ANY = pl.BlockSpec(memory_space=pl.ANY)


def place():
    seq = lax.axis_index("seq")
    head = lax.axis_index("head")
    return seq // ROW, seq % ROW, head // 2, head % 2


def remote(src, dst, send_sem, recv_sem, device):
    return pltpu.make_async_remote_copy(
        src_ref=src,
        dst_ref=dst,
        send_sem=send_sem,
        recv_sem=recv_sem,
        device_id=device,
        device_id_type=MESH,
    )


def row_partner(k):
    y, x, z, c = place()
    device = (y * ROW + 2 * c + k, 2 * z + x // 2)
    return device, (x // 2 == c) & (x % 2 == k)


def signal_row_partners(barrier):
    for k in range(2):
        device, own = row_partner(k)

        @pl.when(jnp.logical_not(own))
        def _(device=device):
            pl.semaphore_signal(barrier, inc=1, device_id=device, device_id_type=MESH)


def row_partner_count():
    y, x, z, c = place()
    return 2 - (x // 2 == c).astype(jnp.int32)


def row_start(src, dst, send_sem, recv_sem, k):
    device, own = row_partner(k)

    @pl.when(jnp.logical_not(own))
    def _():
        remote(src, dst, send_sem, recv_sem, device).start()

    @pl.when(own)
    def _():
        pltpu.make_async_copy(src, dst, recv_sem).start()


def row_wait_recv(dst, recv_sem):
    pltpu.make_async_copy(dst, dst, recv_sem).wait()


def row_wait_send(src, dst, send_sem, recv_sem, k):
    device, own = row_partner(k)

    @pl.when(jnp.logical_not(own))
    def _():
        remote(src, dst, send_sem, recv_sem, device).wait_send()


def neighbours():
    y, x, z, c = place()
    up = (lax.rem(y + 1, ROW) * ROW + x, 2 * z + c)
    down = (lax.rem(y + ROW - 1, ROW) * ROW + x, 2 * z + c)
    sibling = (y * ROW + x, 2 * z + 1 - c)
    return up, down, sibling


def meet(others):
    barrier = pltpu.get_barrier_semaphore()
    signal_row_partners(barrier)
    for device in others:
        pl.semaphore_signal(barrier, inc=1, device_id=device, device_id_type=MESH)
    pl.semaphore_wait(barrier, row_partner_count() + len(others))


def gather_kernel(
    q, k, v, do, sel, qn, kn, vn, don, seln,
    row_send, row_recv, ring_send, ring_recv, far_send, far_recv, sib_send, sib_recv,
):
    y, x, z, c = place()
    up, down, sibling = neighbours()
    meet(neighbours())
    odd = x % 2
    home = pl.multiple_of((2 * y + x // 2) * EIGHTH + odd * PIECE, PIECE)
    spot = pl.multiple_of(odd * PIECE, PIECE)

    def row_refs(t, h):
        cols = pl.ds(h * HEAD, HEAD)
        if t == 0:
            return k.at[:, cols], kn.at[pl.ds(home, PIECE)]
        if t == 1:
            return v.at[:, cols], vn.at[pl.ds(home, PIECE)]
        if t == 2:
            return q.at[:, cols], qn.at[pl.ds(spot, PIECE)]
        if t == 3:
            return do.at[:, cols], don.at[pl.ds(spot, PIECE)]
        return sel.at[h], seln.at[odd]

    for t in range(5):
        for h in range(2):
            src, dst = row_refs(t, h)
            row_start(src, dst, row_send.at[t, h], row_recv.at[t, odd], h)

    kv = (kn, vn)

    def piece(t, shift, core, j):
        quarter = lax.rem(y + shift + ROW, ROW)
        start = pl.multiple_of((2 * quarter + core) * EIGHTH + j * PIECE, PIECE)
        return kv[t].at[pl.ds(start, PIECE)]

    def sib_copy(t, m, shift, j):
        own = piece(t, shift, c, j)
        return remote(own, own, sib_send.at[t, m, j], sib_recv.at[t, m, j], sibling)

    def ring_copy(t, way, j):
        own = piece(t, 0, c, j)
        return remote(
            own, own, ring_send.at[t, way, j], ring_recv.at[t, way, j], (up, down)[way]
        )

    def far_copy(t, way):
        own = piece(t, (-1, 1)[way], c, way)
        return remote(own, own, far_send.at[t, way], far_recv.at[t, way], (up, down)[way])

    for t in range(2):
        for j in range(2):
            row_wait_recv(piece(t, 0, c, j), row_recv.at[t, j])
            ring_copy(t, j, j).start()
            ring_copy(t, 1 - j, j).start()
            sib_copy(t, 0, 0, j).start()
    for t in range(2):
        for way in range(2):
            ring_copy(t, way, way).wait_recv()
            far_copy(t, way).start()
            sib_copy(t, 1 + way, (-1, 1)[way], way).start()
        for way in range(2):
            ring_copy(t, way, 1 - way).wait_recv()
            sib_copy(t, 1 + way, (-1, 1)[way], 1 - way).start()
    for t in range(2):
        for way in range(2):
            far_copy(t, way).wait_recv()
            sib_copy(t, 3, 2, way).start()
    for t in range(2, 5):
        for j in range(2):
            if t == 2:
                dst = qn.at[pl.ds(j * PIECE, PIECE)]
            elif t == 3:
                dst = don.at[pl.ds(j * PIECE, PIECE)]
            else:
                dst = seln.at[j]
            row_wait_recv(dst, row_recv.at[t, j])
    for t in range(5):
        for h in range(2):
            src, dst = row_refs(t, h)
            row_wait_send(src, dst, row_send.at[t, h], row_recv.at[t, odd], h)
    for t in range(2):
        for way in range(2):
            far_copy(t, way).wait_send()
            for j in range(2):
                ring_copy(t, way, j).wait_send()
        for m, shift in enumerate((0, -1, 1, 2)):
            for j in range(2):
                copy = sib_copy(t, m, shift, j)
                copy.wait_send()
                copy.wait_recv()


def gather(q, k, v, do, sel):
    half = jax.ShapeDtypeStruct((EIGHTH, HEAD), jnp.bfloat16)
    whole = jax.ShapeDtypeStruct((ALL_BLOCKS * BLOCK, HEAD), jnp.bfloat16)
    dma = pltpu.SemaphoreType.DMA
    return pl.pallas_call(
        gather_kernel,
        name="gather",
        out_shape=(half, whole, whole, half, jax.ShapeDtypeStruct((2, 8, 128), jnp.int32)),
        in_specs=[ANY] * 5,
        out_specs=(ANY,) * 5,
        scratch_shapes=[
            dma((5, 2)), dma((5, 2)), dma((2, 2, 2)), dma((2, 2, 2)),
            dma((2, 2)), dma((2, 2)), dma((2, 4, 2)), dma((2, 4, 2)),
        ],
        compiler_params=pltpu.CompilerParams(collective_id=0, has_side_effects=True),
        cost_estimate=pl.CostEstimate(flops=0, bytes_accessed=100_000_000, transcendentals=0),
    )(q, k, v, do, sel)


def dot(a, b, contract):
    return lax.dot_general(a, b, (contract, ((), ())), preferred_element_type=jnp.float32)


def attention_kernel(
    sel, q, do, k, v, out, dq, dk, dv, dk_sum, dv_sum, scores, expons
):
    y, x, z, c = place()
    scaling = 1.0 / math.sqrt(HEAD)
    factor = scaling * math.log2(math.e)

    @pl.loop(0, ALL_BLOCKS)
    def _(block):
        dk_sum[block] = jnp.zeros((BLOCK, HEAD), jnp.float32)
        dv_sum[block] = jnp.zeros((BLOCK, HEAD), jnp.float32)

    @pl.loop(0, ITEMS)
    def _(item):
        block = 8 * y + 4 * c + item
        rows = pl.ds(pl.multiple_of(item * BLOCK, BLOCK), BLOCK)
        query = q[rows, :]
        grad = do[rows, :]
        query_t = query.T
        grad_t = grad.T.astype(jnp.float32)
        ids = [block] + [sel[item // 2, item % 2, t] for t in range(SLOTS - 1)]
        top = jnp.full((1, BLOCK), -1e30, jnp.float32)
        for t in range(SLOTS):
            s = dot(k[ids[t]], query_t, ((1,), (0,)))
            if t == 0:
                key_at = lax.broadcasted_iota(jnp.int32, (BLOCK, BLOCK), 0)
                query_at = lax.broadcasted_iota(jnp.int32, (BLOCK, BLOCK), 1)
                s = jnp.where(key_at <= query_at, s, -1e30)
            else:
                s = jnp.where(ids[t] < block, s, -1e30)
            scores[t] = s
            top = jnp.maximum(top, jnp.max(s, axis=0, keepdims=True))
        top = top * factor
        total = jnp.zeros((1, BLOCK), jnp.float32)
        out_t = jnp.zeros((HEAD, BLOCK), jnp.float32)
        for t in range(SLOTS):
            e = jnp.exp2(scores[t] * factor - top)
            total = total + jnp.sum(e, axis=0, keepdims=True)
            eb = e.astype(jnp.bfloat16)
            expons[t] = eb
            out_t = out_t + dot(v[ids[t]], eb, ((0,), (0,)))
        inverse = 1.0 / total
        out_t = (out_t * inverse).astype(jnp.bfloat16)
        out[rows, :] = out_t.T
        delta = jnp.sum(grad_t * out_t.astype(jnp.float32), axis=0, keepdims=True) * inverse
        scaled_t = (grad_t * inverse).astype(jnp.bfloat16)
        scaled = scaled_t.T
        dq_t = jnp.zeros((HEAD, BLOCK), jnp.float32)
        for t in range(SLOTS):
            eb = expons[t]
            dp = dot(v[ids[t]], scaled_t, ((1,), (0,)))
            ds = (eb.astype(jnp.float32) * (dp - delta)).astype(jnp.bfloat16)
            dq_t = dq_t + dot(k[ids[t]], ds, ((0,), (0,)))
            dk_sum[ids[t]] += dot(ds, query, ((1,), (0,)))
            dv_sum[ids[t]] += dot(eb, scaled, ((1,), (0,)))
        dq[rows, :] = (dq_t * scaling).astype(jnp.bfloat16).T

    @pl.loop(0, ALL_BLOCKS)
    def _(block):
        dk[block] = (dk_sum[block] * scaling).astype(jnp.bfloat16)
        dv[block] = dv_sum[block].astype(jnp.bfloat16)


def attention(sel, q, do, k, v):
    half = jax.ShapeDtypeStruct((EIGHTH, HEAD), jnp.bfloat16)
    blocks = jax.ShapeDtypeStruct((ALL_BLOCKS, BLOCK, HEAD), jnp.bfloat16)
    vmem = pl.BlockSpec(memory_space=pltpu.VMEM)
    return pl.pallas_call(
        attention_kernel,
        name="attention",
        out_shape=(half, half, blocks, blocks),
        in_specs=[pl.BlockSpec(memory_space=pltpu.SMEM)] + [vmem] * 4,
        out_specs=(vmem,) * 4,
        scratch_shapes=[
            pltpu.VMEM((ALL_BLOCKS, BLOCK, HEAD), jnp.float32),
            pltpu.VMEM((ALL_BLOCKS, BLOCK, HEAD), jnp.float32),
            pltpu.VMEM((SLOTS, BLOCK, BLOCK), jnp.float32),
            pltpu.VMEM((SLOTS, BLOCK, BLOCK), jnp.bfloat16),
        ],
        compiler_params=pltpu.CompilerParams(vmem_limit_bytes=VMEM_LIMIT),
        cost_estimate=pl.CostEstimate(
            flops=8_000_000_000, bytes_accessed=20_000_000, transcendentals=5_000_000
        ),
    )(sel, q, do, k.reshape(ALL_BLOCKS, BLOCK, HEAD), v.reshape(ALL_BLOCKS, BLOCK, HEAD))


def back_refs(src, dst, j):
    y, x, z, c = place()
    cols = pl.ds(pl.multiple_of((x % 2) * HEAD, HEAD), HEAD)
    return src.at[pl.ds(j * PIECE, PIECE)], dst.at[:, cols]


SHIFTS = (0, -1, 1, 2)
STEP = 256
DEPTH = 8
CHUNK = 64


def reduce_kernel(
    out, dq, dk, dv, weight, cotangent,
    projected, dq_home, dk_home, dv_home, weight_grad,
    attn, mine, theirs, near, far, part, part_sib, part_in, chunks, chunk_sum, row_in, col_in,
    row_send, row_recv, load, sib_send, sib_recv, ring_send, ring_recv, far_send, far_recv,
    part_send, part_recv, z_send, z_recv, wx_send, wx_recv, wy_send, wy_recv,
):
    y, x, z, c = place()
    up, down, sibling = neighbours()
    odd = x % 2
    z_next = (y * ROW + x, 2 * lax.rem(z + 1, DEPTH) + c)
    z_last = (y * ROW + x, 2 * lax.rem(z + DEPTH - 1, DEPTH) + c)
    across = [(y * ROW + lax.rem(x + d, ROW), 2 * z + c) for d in range(1, ROW)]
    along = [(lax.rem(y + d, ROW) * ROW + x, 2 * z + c) for d in range(1, ROW)]
    meet([up, down, sibling, z_next, z_last, along[1]] + across)
    parts = (dk, dv)
    homes = (dk_home, dv_home, dq_home, attn)
    sources = (mine.at[0, 0], mine.at[1, 0], dq, out)

    def go_home(t, j):
        src, dst = back_refs(sources[t], homes[t], j)
        row_start(src, dst, row_send.at[t, j], row_recv.at[t, odd], j)

    def eighth(t, shift, core):
        quarter = lax.rem(y + shift + ROW, ROW)
        start = pl.multiple_of((2 * quarter + core) * EIGHTH, EIGHTH)
        return parts[t].at[pl.ds(start, EIGHTH)]

    def load_copy(t, m):
        return pltpu.make_async_copy(eighth(t, SHIFTS[m], c), mine.at[t, m], load.at[t, m])

    def sib_copy(t, m):
        return remote(
            eighth(t, SHIFTS[m], 1 - c), theirs.at[t, m],
            sib_send.at[t, m], sib_recv.at[t, m], sibling,
        )

    def half(ref, j):
        return ref.at[pl.ds(j * PIECE, PIECE)]

    def far_copy(t, way):
        return remote(
            half(mine.at[t, 3], way), far.at[t, way],
            far_send.at[t, way], far_recv.at[t, way], (up, down)[way],
        )

    def ring_copy(t, way, j):
        return remote(
            half(mine.at[t, 2 - way], j), near.at[t, way, j],
            ring_send.at[t, way, j], ring_recv.at[t, way, j], (up, down)[way],
        )

    def add_theirs(t, m):
        load_copy(t, m).wait()
        sib_copy(t, m).wait_recv()

        @pl.loop(0, EIGHTH // STEP)
        def _(i):
            rows = pl.ds(pl.multiple_of(i * STEP, STEP), STEP)
            total = mine[t, m, rows, :].astype(jnp.float32)
            total = total + theirs[t, m, rows, :].astype(jnp.float32)
            mine[t, m, rows, :] = total.astype(jnp.bfloat16)

    def add_far(t, way):
        far_copy(t, way).wait_recv()

        @pl.loop(0, PIECE // STEP)
        def _(i):
            there = pl.ds(pl.multiple_of(i * STEP, STEP), STEP)
            here = pl.ds(pl.multiple_of(way * PIECE + i * STEP, STEP), STEP)
            total = mine[t, 2 - way, here, :].astype(jnp.float32)
            total = total + far[t, way, there, :].astype(jnp.float32)
            mine[t, 2 - way, here, :] = total.astype(jnp.bfloat16)

        ring_copy(t, way, way).start()

    def finish(t, j):
        for way in range(2):
            ring_copy(t, way, j).wait_recv()

        @pl.loop(0, PIECE // STEP)
        def _(i):
            there = pl.ds(pl.multiple_of(i * STEP, STEP), STEP)
            here = pl.ds(pl.multiple_of(j * PIECE + i * STEP, STEP), STEP)
            total = mine[t, 0, here, :].astype(jnp.float32)
            total = total + theirs[t, 0, here, :].astype(jnp.float32)
            total = total + near[t, 0, j, there, :].astype(jnp.float32)
            total = total + near[t, 1, j, there, :].astype(jnp.float32)
            mine[t, 0, here, :] = total.astype(jnp.bfloat16)

        go_home(t, j)

    def part_copy():
        return remote(part.at[:, 1 - c], part_sib, part_send, part_recv, sibling)

    def z_at(shift):
        return lax.rem(z + shift + DEPTH, DEPTH)

    def z_copy(way, step):
        src = part.at[z_at(step if way == 0 else -step), c]
        dst = part_in.at[way, step - 1]
        if step == DEPTH // 2:
            rows = pl.ds(way * (CHUNK // 2), CHUNK // 2)
            src, dst = src.at[rows], dst.at[rows]
        return remote(
            src, dst, z_send.at[way, step - 1], z_recv.at[way, step - 1], (z_next, z_last)[way]
        )

    def z_step(step):
        for way in range(2):
            z_copy(way, step + 1).wait_recv()
            mine_at = z_at(step if way == 0 else -step)
            rows = pl.ds(0, CHUNK)
            if step + 1 == DEPTH // 2:
                rows = pl.ds(way * (CHUNK // 2), CHUNK // 2)
            total = part[mine_at, c, rows, :].astype(jnp.float32)
            total = total + part_in[way, step, rows, :].astype(jnp.float32)
            part[mine_at, c, rows, :] = total.astype(jnp.bfloat16)
            z_copy(way, step).start()

    def project():
        @pl.loop(0, 4)
        def _(i):
            rows = pl.ds(pl.multiple_of(i * 256, 256), 256)
            for n in range(4):
                cols = pl.ds(n * 512, 512)
                tile = dot(attn[rows, :], weight[:, cols], ((1,), (0,))).astype(jnp.bfloat16)
                for a in range(2):
                    for b in range(2):
                        at = (2 * a + b) * CHUNK
                        part[2 * i + a, b, :, cols] = tile[at : at + CHUNK, :]

        part_copy().start()

    def project_sum():
        part_copy().wait()

        @pl.loop(0, DEPTH)
        def _(i):
            total = part[i, c].astype(jnp.float32) + part_sib[i].astype(jnp.float32)
            part[i, c] = total.astype(jnp.bfloat16)

        for way in range(2):
            z_copy(way, DEPTH // 2).start()

    def project_end():
        total = part[z, c].astype(jnp.float32)
        for way in range(2):
            z_copy(way, 1).wait_recv()
            total = total + part_in[way, 0].astype(jnp.float32)
        projected[...] = total.astype(jnp.bfloat16)

    def across_copy(d):
        return remote(
            chunks.at[lax.rem(x + d, ROW)], row_in.at[d - 1],
            wx_send.at[d - 1], wx_recv.at[d - 1], across[d - 1],
        )

    def along_copy(d):
        return remote(
            chunk_sum.at[lax.rem(y + d, ROW)], col_in.at[d - 1],
            wy_send.at[d - 1], wy_recv.at[d - 1], along[d - 1],
        )

    def weight_start():
        attn_t = attn[...].T
        for yy in range(ROW):
            tile = dot(attn_t, cotangent[:, yy * 512 : (yy + 1) * 512], ((1,), (0,)))
            for xx in range(ROW):
                chunks[xx, yy] = tile[:, xx * 128 : (xx + 1) * 128].astype(jnp.bfloat16)
        for d in range(1, ROW):
            across_copy(d).start()

    def weight_middle():
        for d in range(1, ROW):
            across_copy(d).wait_recv()
        for yy in range(ROW):
            total = chunks[x, yy].astype(jnp.float32)
            for d in range(ROW - 1):
                total = total + row_in[d, yy].astype(jnp.float32)
            chunk_sum[yy] = total.astype(jnp.bfloat16)
        for d in range(1, ROW):
            along_copy(d).start()

    def weight_end():
        total = chunk_sum[y].astype(jnp.float32)
        for d in range(1, ROW):
            along_copy(d).wait_recv()
            total = total + col_in[d - 1].astype(jnp.float32)
        weight_grad[...] = total

    for j in range(2):
        go_home(3, j)
    for m in (3, 1, 2, 0):
        for t in range(2):
            sib_copy(t, m).start()
            load_copy(t, m).start()
    for j in range(2):
        go_home(2, j)

    for t in range(2):
        add_theirs(t, 3)
        for way in range(2):
            far_copy(t, way).start()
    for h in range(2):
        row_wait_recv(attn.at[:, pl.ds(h * HEAD, HEAD)], row_recv.at[3, h])
    project()
    for t in range(2):
        for way in range(2):
            add_theirs(t, 2 - way)
            ring_copy(t, way, 1 - way).start()
    project_sum()
    weight_start()
    for way in range(2):
        add_far(0, way)
    z_step(3)
    for way in range(2):
        add_far(1, way)
    weight_middle()
    z_step(2)
    for t in range(2):
        load_copy(t, 0).wait()
        sib_copy(t, 0).wait_recv()
    finish(0, 0)
    z_step(1)
    finish(0, 1)
    project_end()
    weight_end()
    finish(1, 0)
    finish(1, 1)

    for t in range(4):
        if t < 3:
            for h in range(2):
                row_wait_recv(homes[t].at[:, pl.ds(h * HEAD, HEAD)], row_recv.at[t, h])
        for j in range(2):
            src, dst = back_refs(sources[t], homes[t], j)
            row_wait_send(src, dst, row_send.at[t, j], row_recv.at[t, odd], j)
    for t in range(2):
        for m in range(4):
            sib_copy(t, m).wait_send()
        for way in range(2):
            far_copy(t, way).wait_send()
            for j in range(2):
                ring_copy(t, way, j).wait_send()
    for step in range(1, DEPTH // 2 + 1):
        for way in range(2):
            z_copy(way, step).wait_send()
    for d in range(1, ROW):
        across_copy(d).wait_send()
        along_copy(d).wait_send()


def reduce_home(out, dq, dk, dv, weight, cotangent):
    home = jax.ShapeDtypeStruct((PIECE, 2 * HEAD), jnp.bfloat16)
    dma = pltpu.SemaphoreType.DMA
    vmem = pl.BlockSpec(memory_space=pltpu.VMEM)
    wide = weight.shape[1]
    bf16 = jnp.bfloat16
    return pl.pallas_call(
        reduce_kernel,
        name="reduce_home",
        out_shape=(
            jax.ShapeDtypeStruct((CHUNK, wide), bf16),
            home, home, home,
            jax.ShapeDtypeStruct((2 * HEAD, HEAD), jnp.float32),
        ),
        in_specs=[ANY] * 4 + [vmem] * 2,
        out_specs=(vmem, ANY, ANY, ANY, vmem),
        scratch_shapes=[
            pltpu.VMEM((PIECE, 2 * HEAD), bf16),
            pltpu.VMEM((2, 4, EIGHTH, HEAD), bf16),
            pltpu.VMEM((2, 4, EIGHTH, HEAD), bf16),
            pltpu.VMEM((2, 2, 2, PIECE, HEAD), bf16),
            pltpu.VMEM((2, 2, PIECE, HEAD), bf16),
            pltpu.VMEM((DEPTH, 2, CHUNK, wide), bf16),
            pltpu.VMEM((DEPTH, CHUNK, wide), bf16),
            pltpu.VMEM((2, DEPTH // 2, CHUNK, wide), bf16),
            pltpu.VMEM((ROW, ROW, 2 * HEAD, HEAD), bf16),
            pltpu.VMEM((ROW, 2 * HEAD, HEAD), bf16),
            pltpu.VMEM((ROW - 1, ROW, 2 * HEAD, HEAD), bf16),
            pltpu.VMEM((ROW - 1, 2 * HEAD, HEAD), bf16),
            dma((4, 2)), dma((4, 2)), dma((2, 4)), dma((2, 4)), dma((2, 4)),
            dma((2, 2, 2)), dma((2, 2, 2)), dma((2, 2)), dma((2, 2)),
            dma, dma, dma((2, 4)), dma((2, 4)), dma((3,)), dma((3,)), dma((3,)), dma((3,)),
        ],
        compiler_params=pltpu.CompilerParams(
            collective_id=2, has_side_effects=True, vmem_limit_bytes=VMEM_LIMIT
        ),
        cost_estimate=pl.CostEstimate(flops=0, bytes_accessed=150_000_000, transcendentals=0),
    )(out, dq, dk.reshape(-1, HEAD), dv.reshape(-1, HEAD), weight, cotangent)


def settle_kernel(*refs):
    count = len(refs) // 2
    for i in range(count):
        refs[count + i][...] = refs[i][...]


def settle(*arrays):
    vmem = pl.BlockSpec(memory_space=pltpu.VMEM)
    return pl.pallas_call(
        settle_kernel,
        name="settle",
        out_shape=tuple(jax.ShapeDtypeStruct(a.shape, a.dtype) for a in arrays),
        in_specs=[vmem] * len(arrays),
        out_specs=(vmem,) * len(arrays),
        compiler_params=pltpu.CompilerParams(vmem_limit_bytes=VMEM_LIMIT),
    )(*arrays)


def shards(queries, key_states, values, selection, out_weight, cotangent):
    grad_attn = dot(cotangent, out_weight, ((1,), (1,))).astype(jnp.bfloat16)
    sel = jnp.pad(selection, ((0, 0), (0, 6), (0, 124)))
    q, k, v, do, sel = gather(queries, key_states, values, grad_attn, sel)
    out, dq, dk, dv = attention(sel, q, do, k, v)
    return settle(*reduce_home(out, dq, dk, dv, out_weight, cotangent))


def solution(mesh):
    in_specs = (
        P("seq", "head"),
        P("seq", "head"),
        P("seq", "head"),
        P("head", "seq", None),
        P("head", None),
        P("seq", None),
    )
    out_specs = (
        P(("seq", "head"), None),
        P("seq", "head"),
        P("seq", "head"),
        P("seq", "head"),
        P("head", "seq"),
    )
    return jax.shard_map(shards, mesh=mesh, in_specs=in_specs, out_specs=out_specs, check_vma=False)
```

```python
import math

import jax
import jax.numpy as jnp
from jax import lax
from jax.experimental import pallas as pl
from jax.experimental.pallas import tpu as pltpu
from jax.sharding import PartitionSpec as P

ROW = 4
DEPTH = 8
HEAD = 128
BLOCK = 512
ITEMS = 4
SLOTS = 5
ALL_BLOCKS = 32
CHUNK = 64
SHIFTS = (0, -1, 1, 2)
SCALING = 1.0 / math.sqrt(HEAD)
FACTOR = SCALING * math.log2(math.e)
MESH = pl.DeviceIdType.MESH
VMEM_LIMIT = 62 * 1024 * 1024
ANY = pl.BlockSpec(memory_space=pl.ANY)


def place():
    seq = lax.axis_index("seq")
    head = lax.axis_index("head")
    return seq // ROW, seq % ROW, head // 2, head % 2


def remote(src, dst, send_sem, recv_sem, device):
    return pltpu.make_async_remote_copy(
        src_ref=src,
        dst_ref=dst,
        send_sem=send_sem,
        recv_sem=recv_sem,
        device_id=device,
        device_id_type=MESH,
    )


def row_partner(k):
    y, x, z, c = place()
    device = (y * ROW + 2 * c + k, 2 * z + x // 2)
    return device, (x // 2 == c) & (x % 2 == k)


def row_start(src, dst, send_sem, recv_sem, k):
    device, own = row_partner(k)

    @pl.when(jnp.logical_not(own))
    def _():
        remote(src, dst, send_sem, recv_sem, device).start()

    @pl.when(own)
    def _():
        pltpu.make_async_copy(src, dst, recv_sem).start()


def row_wait_recv(dst, recv_sem):
    pltpu.make_async_copy(dst, dst, recv_sem).wait()


def row_wait_send(src, dst, send_sem, recv_sem, k):
    device, own = row_partner(k)

    @pl.when(jnp.logical_not(own))
    def _():
        remote(src, dst, send_sem, recv_sem, device).wait_send()


def meet(others):
    y, x, z, c = place()
    barrier = pltpu.get_barrier_semaphore()
    for k in range(2):
        device, own = row_partner(k)

        @pl.when(jnp.logical_not(own))
        def _(device=device):
            pl.semaphore_signal(barrier, inc=1, device_id=device, device_id_type=MESH)

    for device in others:
        pl.semaphore_signal(barrier, inc=1, device_id=device, device_id_type=MESH)
    pl.semaphore_wait(barrier, 2 - (x // 2 == c).astype(jnp.int32) + len(others))


def dot(a, b, contract):
    return lax.dot_general(a, b, (contract, ((), ())), preferred_element_type=jnp.float32)


def layer_kernel(
    q_in, k_in, v_in, sel_in, weight_in, cot_in,
    projected, dq_home, dk_home, dv_home, weight_grad, sel_land,
    k_own, v_own, weight, cot, sel, qn, kn, vn, don, scaled, expons, terms, stats,
    parts, theirs, near, far, attn, part, part_sib, part_in, chunks, chunk_sum, row_in, col_in,
    load, sel_sem, row_send, row_recv, kv_send, kv_recv, kv_far_send, kv_far_recv,
    kv_sib_send, kv_sib_recv, home_send, home_recv, sib_send, sib_recv,
    ring_send, ring_recv, far_send, far_recv,
    part_send, part_recv, z_send, z_recv, wx_send, wx_recv, wy_send, wy_recv,
):
    y, x, z, c = place()
    odd = x % 2
    f32, bf16 = jnp.float32, jnp.bfloat16
    up = (lax.rem(y + 1, ROW) * ROW + x, 2 * z + c)
    down = (lax.rem(y + ROW - 1, ROW) * ROW + x, 2 * z + c)
    sibling = (y * ROW + x, 2 * z + 1 - c)
    z_next = (y * ROW + x, 2 * lax.rem(z + 1, DEPTH) + c)
    z_last = (y * ROW + x, 2 * lax.rem(z + DEPTH - 1, DEPTH) + c)
    across = [(y * ROW + lax.rem(x + d, ROW), 2 * z + c) for d in range(1, ROW)]
    along = [(lax.rem(y + d, ROW) * ROW + x, 2 * z + c) for d in range(1, ROW)]

    loads = [
        pltpu.make_async_copy(src, dst, load.at[i])
        for i, (src, dst) in enumerate(
            ((k_in, k_own), (v_in, v_own), (cot_in, cot), (weight_in, weight))
        )
    ]
    for copy in loads:
        copy.start()
    meet([up, down, sibling, z_next, z_last, along[1]] + across)

    home_at = 4 * (2 * y + x // 2) + 2 * odd

    def row_refs(t, h):
        cols = pl.ds(h * HEAD, HEAD)
        if t == 0:
            return k_own.at[:, :, cols], kn.at[pl.ds(home_at, 2)]
        if t == 1:
            return q_in.at[:, :, cols], qn.at[pl.ds(2 * odd, 2)]
        if t == 2:
            return v_own.at[:, :, cols], vn.at[pl.ds(home_at, 2)]
        if t == 3:
            return k_own.at[:, :, cols], don.at[pl.ds(2 * odd, 2)]
        return sel_in.at[h], sel_land.at[odd]

    def row_go(t):
        for h in range(2):
            src, dst = row_refs(t, h)
            row_start(src, dst, row_send.at[t, h], row_recv.at[t, odd], h)

    def row_sent(t):
        for h in range(2):
            src, dst = row_refs(t, h)
            row_wait_send(src, dst, row_send.at[t, h], row_recv.at[t, odd], h)

    def row_arrive(t, j):
        if t == 1:
            dst = qn.at[pl.ds(2 * j, 2)]
        elif t == 3:
            dst = don.at[pl.ds(2 * j, 2)]
        elif t == 4:
            dst = sel_land.at[j]
        else:
            dst = piece(t // 2, 0, c, j)
        row_wait_recv(dst, row_recv.at[t, j])

    def piece(t, shift, core, j):
        quarter = lax.rem(y + shift + ROW, ROW)
        return (kn, vn)[t].at[pl.ds(4 * (2 * quarter + core) + 2 * j, 2)]

    def kv_sib(t, m, j):
        own = piece(t, SHIFTS[m], c, j)
        return remote(own, own, kv_sib_send.at[t, m, j], kv_sib_recv.at[t, m, j], sibling)

    def kv_ring(t, way, j):
        own = piece(t, 0, c, j)
        return remote(own, own, kv_send.at[t, way, j], kv_recv.at[t, way, j], (up, down)[way])

    def kv_far(t, way):
        own = piece(t, (-1, 1)[way], c, way)
        return remote(
            own, own, kv_far_send.at[t, way], kv_far_recv.at[t, way], (up, down)[way]
        )

    def kv_begin(t):
        for j in range(2):
            row_arrive(2 * t, j)
            kv_ring(t, j, j).start()
            kv_ring(t, 1 - j, j).start()
            kv_sib(t, 0, j).start()

    def kv_relay(t):
        for way in range(2):
            kv_ring(t, way, way).wait_recv()
            kv_far(t, way).start()
            kv_sib(t, 1 + way, way).start()

    def kv_rest(t):
        for way in range(2):
            kv_ring(t, way, 1 - way).wait_recv()
            kv_sib(t, 1 + way, 1 - way).start()

    def kv_last(t):
        for way in range(2):
            kv_far(t, way).wait_recv()
            kv_sib(t, 3, way).start()

    def kv_end(t):
        for m in range(4):
            for j in range(2):
                kv_sib(t, m, j).wait_recv()

    def gradient_rows(lo, hi):
        @pl.loop(lo, hi)
        def _(i):
            rows = pl.ds(pl.multiple_of((i % 2) * 256, 256), 256)
            tile = dot(cot[i // 2, rows, :], weight[...], ((1,), (1,)))
            k_own[i // 2, rows, :] = tile.astype(bf16)

    out, dq = don, scaled

    def item_ids(item):
        block = 8 * y + 4 * c + item
        return block, [sel[item // 2, item % 2, t] for t in range(SLOTS - 1)]

    def weigh(lo, hi):
        @pl.loop(lo, hi)
        def _(item):
            block, ids = item_ids(item)
            query_t = qn[item].T
            top = jnp.full((1, BLOCK), -1e30, f32)
            for t in range(SLOTS):
                if t == 0:
                    s = dot(kn[block], query_t, ((1,), (0,)))
                    key_at = lax.broadcasted_iota(jnp.int32, (BLOCK, BLOCK), 0)
                    query_at = lax.broadcasted_iota(jnp.int32, (BLOCK, BLOCK), 1)
                    s = jnp.where(key_at <= query_at, s, -1e30)
                else:
                    s = dot(kn[ids[t - 1]], query_t, ((1,), (0,)))
                    s = jnp.where(ids[t - 1] < block, s, -1e30)
                for n in range(ITEMS):
                    terms[n, t] = s[:, n * HEAD : (n + 1) * HEAD]
                top = jnp.maximum(top, jnp.max(s, axis=0, keepdims=True))
            top = top * FACTOR
            total = jnp.zeros((1, BLOCK), f32)
            for t in range(SLOTS):
                s = jnp.concatenate([terms[n, t] for n in range(ITEMS)], axis=1)
                e = jnp.exp2(s * FACTOR - top)
                total = total + jnp.sum(e, axis=0, keepdims=True)
                expons[item, t] = e.astype(bf16)
            stats[item] = 1.0 / total

    def value_terms():
        @pl.loop(0, ITEMS)
        def _(item):
            scaled_t = (don[item].T.astype(f32) * stats[item]).astype(bf16)
            scaled[item] = scaled_t.T
            rows = scaled[item]
            for t in range(SLOTS):
                terms[item, t] = dot(expons[item, t], rows, ((1,), (0,)))

    def attend():
        @pl.loop(0, ITEMS)
        def _(item):
            block, ids = item_ids(item)
            out_t = dot(vn[block], expons[item, 0], ((0,), (0,)))
            for t in range(1, SLOTS):
                out_t = out_t + dot(vn[ids[t - 1]], expons[item, t], ((0,), (0,)))
            out_t = (out_t * stats[item]).astype(bf16)
            product = don[item].T.astype(f32) * out_t.astype(f32)
            out[item] = out_t.T
            stats[item] = jnp.sum(product, axis=0, keepdims=True) * stats[item]

    def backward(lo, hi):
        @pl.loop(lo, hi)
        def _(item):
            block, ids = item_ids(item)
            query = qn[item]
            scaled_t = scaled[item].T
            delta = stats[item]
            dq_t = jnp.zeros((HEAD, BLOCK), f32)
            for t in range(SLOTS):
                at = block if t == 0 else ids[t - 1]
                dp = dot(vn[at], scaled_t, ((1,), (0,)))
                ds = (expons[item, t].astype(f32) * (dp - delta)).astype(bf16)
                dq_t = dq_t + dot(kn[at], ds, ((0,), (0,)))
                terms[item, t] = dot(ds, query, ((1,), (0,)))
            dq[item] = (dq_t * SCALING).astype(bf16).T

    def gather_terms(t, m):
        @pl.loop(0, 8)
        def _(i):
            target = 8 * lax.rem(y + SHIFTS[m] + ROW, ROW) + i
            total = jnp.zeros((BLOCK, HEAD), f32)
            for item in range(ITEMS):
                block, ids = item_ids(item)
                slot = jnp.int32(0)
                for s in range(SLOTS - 1):
                    slot = jnp.where(ids[s] == target, s + 1, slot)
                slot = jnp.where(target == block, 0, slot)
                chosen = (target == block) | (slot > 0)
                total = total + jnp.where(chosen, terms[item, slot], 0.0)
            if t == 0:
                total = total * SCALING
            parts[t, m, i // 4, i % 4] = total.astype(bf16)

    homes = (dk_home, dv_home, dq_home, attn)
    sources = (parts.at[0, 0, c], parts.at[1, 0, c], dq, out)

    def home_refs(t, j):
        cols = pl.ds(pl.multiple_of(odd * HEAD, HEAD), HEAD)
        return sources[t].at[pl.ds(2 * j, 2)], homes[t].at[:, :, cols]

    def go_home(t, j):
        src, dst = home_refs(t, j)
        row_start(src, dst, home_send.at[t, j], home_recv.at[t, odd], j)

    def come_home(t):
        for h in range(2):
            row_wait_recv(homes[t].at[:, :, pl.ds(h * HEAD, HEAD)], home_recv.at[t, h])

    def sib_copy(t, m):
        return remote(
            parts.at[t, m, 1 - c], theirs.at[t, m],
            sib_send.at[t, m], sib_recv.at[t, m], sibling,
        )

    def far_copy(t, way):
        return remote(
            parts.at[t, 3, c, pl.ds(2 * way, 2)], far.at[t, way],
            far_send.at[t, way], far_recv.at[t, way], (up, down)[way],
        )

    def ring_copy(t, way, j):
        return remote(
            parts.at[t, 2 - way, c, pl.ds(2 * j, 2)], near.at[t, way, j],
            ring_send.at[t, way, j], ring_recv.at[t, way, j], (up, down)[way],
        )

    def share(t):
        for m in (3, 1, 2, 0):
            gather_terms(t, m)
            sib_copy(t, m).start()

    def add_theirs(t, m):
        sib_copy(t, m).wait_recv()

        @pl.loop(0, 4)
        def _(i):
            total = parts[t, m, c, i].astype(f32) + theirs[t, m, i].astype(f32)
            parts[t, m, c, i] = total.astype(bf16)

    def back_far(t):
        add_theirs(t, 3)
        for way in range(2):
            far_copy(t, way).start()

    def back_near(t):
        for way in range(2):
            add_theirs(t, 2 - way)
            ring_copy(t, way, 1 - way).start()

    def back_sum(t):
        for way in range(2):
            far_copy(t, way).wait_recv()

            @pl.loop(0, 2)
            def _(i, way=way):
                total = parts[t, 2 - way, c, 2 * way + i].astype(f32)
                total = total + far[t, way, i].astype(f32)
                parts[t, 2 - way, c, 2 * way + i] = total.astype(bf16)

            ring_copy(t, way, way).start()

    def back_end(t):
        sib_copy(t, 0).wait_recv()
        for j in range(2):
            for way in range(2):
                ring_copy(t, way, j).wait_recv()

            @pl.loop(0, 2)
            def _(i, j=j):
                total = parts[t, 0, c, 2 * j + i].astype(f32)
                total = total + theirs[t, 0, 2 * j + i].astype(f32)
                total = total + near[t, 0, j, i].astype(f32)
                total = total + near[t, 1, j, i].astype(f32)
                parts[t, 0, c, 2 * j + i] = total.astype(bf16)

            go_home(t, j)

    def part_copy():
        return remote(part.at[:, 1 - c], part_sib, part_send, part_recv, sibling)

    def z_at(shift):
        return lax.rem(z + shift + DEPTH, DEPTH)

    def z_copy(way, step):
        src = part.at[z_at(step if way == 0 else -step), c]
        dst = part_in.at[way, step - 1]
        if step == DEPTH // 2:
            rows = pl.ds(way * (CHUNK // 2), CHUNK // 2)
            src, dst = src.at[rows], dst.at[rows]
        return remote(
            src, dst, z_send.at[way, step - 1], z_recv.at[way, step - 1], (z_next, z_last)[way]
        )

    def z_step(step):
        for way in range(2):
            z_copy(way, step + 1).wait_recv()
            mine_at = z_at(step if way == 0 else -step)
            rows = pl.ds(0, CHUNK)
            if step + 1 == DEPTH // 2:
                rows = pl.ds(way * (CHUNK // 2), CHUNK // 2)
            total = part[mine_at, c, rows, :].astype(f32)
            total = total + part_in[way, step, rows, :].astype(f32)
            part[mine_at, c, rows, :] = total.astype(bf16)
            z_copy(way, step).start()

    def project():
        @pl.loop(0, 4)
        def _(i):
            rows = pl.ds(pl.multiple_of((i % 2) * 256, 256), 256)
            for n in range(4):
                cols = pl.ds(n * 512, 512)
                tile = dot(attn[i // 2, rows, :], weight[:, cols], ((1,), (0,))).astype(bf16)
                for a in range(2):
                    for b in range(2):
                        at = (2 * a + b) * CHUNK
                        part[2 * i + a, b, :, cols] = tile[at : at + CHUNK, :]

        part_copy().start()

    def project_sum():
        part_copy().wait()

        @pl.loop(0, DEPTH)
        def _(i):
            total = part[i, c].astype(f32) + part_sib[i].astype(f32)
            part[i, c] = total.astype(bf16)

        for way in range(2):
            z_copy(way, DEPTH // 2).start()

    def project_end():
        total = part[z, c].astype(f32)
        for way in range(2):
            z_copy(way, 1).wait_recv()
            total = total + part_in[way, 0].astype(f32)
        projected[...] = total.astype(bf16)

    def across_copy(d):
        return remote(
            chunks.at[lax.rem(x + d, ROW)], row_in.at[d - 1],
            wx_send.at[d - 1], wx_recv.at[d - 1], across[d - 1],
        )

    def along_copy(d):
        return remote(
            chunk_sum.at[lax.rem(y + d, ROW)], col_in.at[d - 1],
            wy_send.at[d - 1], wy_recv.at[d - 1], along[d - 1],
        )

    def weight_start():
        first_t, second_t = attn[0].T, attn[1].T
        for yy in range(ROW):
            cols = slice(yy * 512, (yy + 1) * 512)
            tile = dot(first_t, cot[0, :, cols], ((1,), (0,)))
            tile = tile + dot(second_t, cot[1, :, cols], ((1,), (0,)))
            for xx in range(ROW):
                chunks[xx, yy] = tile[:, xx * 128 : (xx + 1) * 128].astype(bf16)
        for d in range(1, ROW):
            across_copy(d).start()

    def weight_middle():
        for d in range(1, ROW):
            across_copy(d).wait_recv()
        for yy in range(ROW):
            total = chunks[x, yy].astype(f32)
            for d in range(ROW - 1):
                total = total + row_in[d, yy].astype(f32)
            chunk_sum[yy] = total.astype(bf16)
        for d in range(1, ROW):
            along_copy(d).start()

    def weight_end():
        total = chunk_sum[y].astype(f32)
        for d in range(1, ROW):
            along_copy(d).wait_recv()
            total = total + col_in[d - 1].astype(f32)
        weight_grad[...] = total

    loads[0].wait()
    row_go(0)
    loads[1].wait()
    kv_begin(0)
    row_go(2)
    row_sent(0)
    loads[2].wait()
    loads[3].wait()
    gradient_rows(0, 4)
    kv_relay(0)
    row_go(1)
    row_go(4)
    kv_rest(0)
    row_go(3)
    kv_last(0)
    kv_begin(1)
    for j in range(2):
        row_arrive(4, j)
    sel_copy = pltpu.make_async_copy(sel_land, sel, sel_sem)
    sel_copy.start()
    for j in range(2):
        row_arrive(1, j)
    kv_end(0)
    sel_copy.wait()
    weigh(0, 4)
    kv_relay(1)
    kv_rest(1)
    for j in range(2):
        row_arrive(3, j)
    value_terms()
    share(1)
    kv_last(1)
    back_far(1)
    kv_end(1)
    attend()
    for j in range(2):
        go_home(3, j)
    back_near(1)
    backward(0, 1)
    back_sum(1)
    come_home(3)
    project()
    backward(1, 2)
    project_sum()
    backward(2, 3)
    z_step(3)
    backward(3, 4)
    share(0)
    back_far(0)
    for j in range(2):
        go_home(2, j)
    z_step(2)
    back_near(0)
    weight_start()
    back_sum(0)
    z_step(1)
    weight_middle()
    back_end(1)
    project_end()
    weight_end()
    back_end(0)

    for t in range(3):
        come_home(t)
    for t in range(1, 5):
        row_sent(t)
    for t in range(4):
        for j in range(2):
            src, dst = home_refs(t, j)
            row_wait_send(src, dst, home_send.at[t, j], home_recv.at[t, odd], j)
    for t in range(2):
        for m in range(4):
            sib_copy(t, m).wait_send()
            for j in range(2):
                kv_sib(t, m, j).wait_send()
        for way in range(2):
            far_copy(t, way).wait_send()
            kv_far(t, way).wait_send()
            for j in range(2):
                ring_copy(t, way, j).wait_send()
                kv_ring(t, way, j).wait_send()
    for step in range(1, DEPTH // 2 + 1):
        for way in range(2):
            z_copy(way, step).wait_send()
    for d in range(1, ROW):
        across_copy(d).wait_send()
        along_copy(d).wait_send()


def layer(q, k, v, sel, weight, cot):
    f32, bf16 = jnp.float32, jnp.bfloat16
    home = jax.ShapeDtypeStruct((2, BLOCK, 2 * HEAD), bf16)
    dma = pltpu.SemaphoreType.DMA
    vmem = pl.BlockSpec(memory_space=pltpu.VMEM)
    wide = weight.shape[1]
    own = pltpu.VMEM((2, BLOCK, 2 * HEAD), bf16)
    eighth = pltpu.VMEM((ITEMS, BLOCK, HEAD), bf16)
    return pl.pallas_call(
        layer_kernel,
        name="layer",
        out_shape=(
            jax.ShapeDtypeStruct((CHUNK, wide), bf16),
            home, home, home,
            jax.ShapeDtypeStruct((2 * HEAD, HEAD), f32),
            jax.ShapeDtypeStruct(sel.shape, jnp.int32),
        ),
        in_specs=[ANY] * 6,
        out_specs=(vmem, ANY, ANY, ANY, vmem, ANY),
        scratch_shapes=[
            own, own,
            pltpu.VMEM(weight.shape, bf16),
            pltpu.VMEM((2, BLOCK, wide), bf16),
            pltpu.SMEM(sel.shape, jnp.int32),
            eighth,
            pltpu.VMEM((ALL_BLOCKS, BLOCK, HEAD), bf16),
            pltpu.VMEM((ALL_BLOCKS, BLOCK, HEAD), bf16),
            eighth, eighth,
            pltpu.VMEM((ITEMS, SLOTS, BLOCK, BLOCK), bf16),
            pltpu.VMEM((ITEMS, SLOTS, BLOCK, HEAD), f32),
            pltpu.VMEM((ITEMS, 1, BLOCK), f32),
            pltpu.VMEM((2, 4, 2, 4, BLOCK, HEAD), bf16),
            pltpu.VMEM((2, 4, 4, BLOCK, HEAD), bf16),
            pltpu.VMEM((2, 2, 2, 2, BLOCK, HEAD), bf16),
            pltpu.VMEM((2, 2, 2, BLOCK, HEAD), bf16),
            own,
            pltpu.VMEM((DEPTH, 2, CHUNK, wide), bf16),
            pltpu.VMEM((DEPTH, CHUNK, wide), bf16),
            pltpu.VMEM((2, DEPTH // 2, CHUNK, wide), bf16),
            pltpu.VMEM((ROW, ROW, 2 * HEAD, HEAD), bf16),
            pltpu.VMEM((ROW, 2 * HEAD, HEAD), bf16),
            pltpu.VMEM((ROW - 1, ROW, 2 * HEAD, HEAD), bf16),
            pltpu.VMEM((ROW - 1, 2 * HEAD, HEAD), bf16),
            dma((4,)), dma, dma((5, 2)), dma((5, 2)),
            dma((2, 2, 2)), dma((2, 2, 2)), dma((2, 2)), dma((2, 2)),
            dma((2, 4, 2)), dma((2, 4, 2)), dma((4, 2)), dma((4, 2)),
            dma((2, 4)), dma((2, 4)), dma((2, 2, 2)), dma((2, 2, 2)), dma((2, 2)), dma((2, 2)),
            dma, dma, dma((2, 4)), dma((2, 4)), dma((3,)), dma((3,)), dma((3,)), dma((3,)),
        ],
        compiler_params=pltpu.CompilerParams(
            collective_id=0, has_side_effects=True, vmem_limit_bytes=VMEM_LIMIT
        ),
    )(q, k, v, sel, weight, cot)


def settle_kernel(*refs):
    count = len(refs) // 2
    for i in range(count):
        refs[count + i][...] = refs[i][...]


def settle(*arrays):
    vmem = pl.BlockSpec(memory_space=pltpu.VMEM)
    return pl.pallas_call(
        settle_kernel,
        name="settle",
        out_shape=tuple(jax.ShapeDtypeStruct(a.shape, a.dtype) for a in arrays),
        in_specs=[vmem] * len(arrays),
        out_specs=(vmem,) * len(arrays),
        compiler_params=pltpu.CompilerParams(vmem_limit_bytes=VMEM_LIMIT),
    )(*arrays)


def shards(queries, key_states, values, selection, out_weight, cotangent):
    def blocks(array):
        return array.reshape(2, BLOCK, -1)

    results = layer(
        blocks(queries), blocks(key_states), blocks(values), selection, out_weight,
        blocks(cotangent),
    )
    projected, query_grad, key_grad, value_grad, weight_grad = settle(*results[:5])
    query_grad, key_grad, value_grad = (
        g.reshape(queries.shape) for g in (query_grad, key_grad, value_grad)
    )
    return projected, query_grad, key_grad, value_grad, weight_grad


def solution(mesh):
    in_specs = (
        P("seq", "head"),
        P("seq", "head"),
        P("seq", "head"),
        P("head", "seq", None),
        P("head", None),
        P("seq", None),
    )
    out_specs = (
        P(("seq", "head"), None),
        P("seq", "head"),
        P("seq", "head"),
        P("seq", "head"),
        P("head", "seq"),
    )
    return jax.shard_map(shards, mesh=mesh, in_specs=in_specs, out_specs=out_specs, check_vma=False)
```

```python
import math

import jax
import jax.numpy as jnp
from jax import lax
from jax.experimental import pallas as pl
from jax.experimental.pallas import tpu as pltpu
from jax.sharding import PartitionSpec as P

ROW = 4
DEPTH = 8
HEAD = 128
BLOCK = 512
ITEMS = 4
SLOTS = 5
ALL_BLOCKS = 32
CHUNK = 64
STEP = 256
SHIFTS = (0, -1, 1, 2)
SCALING = 1.0 / math.sqrt(HEAD)
FACTOR = SCALING * math.log2(math.e)
MESH = pl.DeviceIdType.MESH
VMEM_LIMIT = 62 * 1024 * 1024
ANY = pl.BlockSpec(memory_space=pl.ANY)


def place():
    seq = lax.axis_index("seq")
    head = lax.axis_index("head")
    return seq // ROW, seq % ROW, head // 2, head % 2


def remote(src, dst, send_sem, recv_sem, device):
    return pltpu.make_async_remote_copy(
        src_ref=src,
        dst_ref=dst,
        send_sem=send_sem,
        recv_sem=recv_sem,
        device_id=device,
        device_id_type=MESH,
    )


def row_partner(k):
    y, x, z, c = place()
    device = (y * ROW + 2 * c + k, 2 * z + x // 2)
    return device, (x // 2 == c) & (x % 2 == k)


def row_start(src, dst, send_sem, recv_sem, k):
    device, own = row_partner(k)

    @pl.when(jnp.logical_not(own))
    def _():
        remote(src, dst, send_sem, recv_sem, device).start()

    @pl.when(own)
    def _():
        pltpu.make_async_copy(src, dst, recv_sem).start()


def row_wait_recv(dst, recv_sem):
    pltpu.make_async_copy(dst, dst, recv_sem).wait()


def row_wait_send(src, dst, send_sem, recv_sem, k):
    device, own = row_partner(k)

    @pl.when(jnp.logical_not(own))
    def _():
        remote(src, dst, send_sem, recv_sem, device).wait_send()


def meet(others):
    y, x, z, c = place()
    barrier = pltpu.get_barrier_semaphore()
    for k in range(2):
        device, own = row_partner(k)

        @pl.when(jnp.logical_not(own))
        def _(device=device):
            pl.semaphore_signal(barrier, inc=1, device_id=device, device_id_type=MESH)

    for device in others:
        pl.semaphore_signal(barrier, inc=1, device_id=device, device_id_type=MESH)
    pl.semaphore_wait(barrier, 2 - (x // 2 == c).astype(jnp.int32) + len(others))


def dot(a, b, contract):
    return lax.dot_general(a, b, (contract, ((), ())), preferred_element_type=jnp.float32)


def layer_kernel(
    q_in, k_in, v_in, sel_in, weight_in, cot_in,
    projected, dq_home, dk_home, dv_home, weight_grad, sel_land,
    k_own, v_own, weight, cot, sel, qn, kn, vn, don, scaled, expons, terms, stats,
    parts, theirs, near, far, attn, part, part_sib, part_in, chunks, chunk_sum, row_in, col_in,
    load, sel_sem, row_send, row_recv, kv_send, kv_recv, kv_far_send, kv_far_recv,
    kv_sib_send, kv_sib_recv, home_send, home_recv, sib_send, sib_recv,
    ring_send, ring_recv, far_send, far_recv,
    part_send, part_recv, z_send, z_recv, wx_send, wx_recv, wy_send, wy_recv,
):
    y, x, z, c = place()
    odd = x % 2
    f32, bf16 = jnp.float32, jnp.bfloat16
    up = (lax.rem(y + 1, ROW) * ROW + x, 2 * z + c)
    down = (lax.rem(y + ROW - 1, ROW) * ROW + x, 2 * z + c)
    sibling = (y * ROW + x, 2 * z + 1 - c)
    z_next = (y * ROW + x, 2 * lax.rem(z + 1, DEPTH) + c)
    z_last = (y * ROW + x, 2 * lax.rem(z + DEPTH - 1, DEPTH) + c)
    across = [(y * ROW + lax.rem(x + d, ROW), 2 * z + c) for d in range(1, ROW)]
    along = [(lax.rem(y + d, ROW) * ROW + x, 2 * z + c) for d in range(1, ROW)]

    loads = [
        pltpu.make_async_copy(src, dst, load.at[i])
        for i, (src, dst) in enumerate(
            ((k_in, k_own), (v_in, v_own), (cot_in, cot), (weight_in, weight))
        )
    ]
    for copy in loads:
        copy.start()
    meet([up, down, sibling, z_next, z_last, along[1]] + across)

    home_at = 4 * (2 * y + x // 2) + 2 * odd

    def row_refs(t, h, b):
        cols = pl.ds(h * HEAD, HEAD)
        if t == 0:
            return k_own.at[pl.ds(b, 1), :, cols], kn.at[pl.ds(home_at + b, 1)]
        if t == 1:
            return q_in.at[:, :, cols], qn.at[pl.ds(2 * odd, 2)]
        if t == 2:
            return v_own.at[pl.ds(b, 1), :, cols], vn.at[pl.ds(home_at + b, 1)]
        if t == 3:
            return k_own.at[:, :, cols], don.at[pl.ds(2 * odd, 2)]
        return sel_in.at[h], sel_land.at[odd]

    def row_go(t, b=0):
        for h in range(2):
            src, dst = row_refs(t, h, b)
            row_start(src, dst, row_send.at[t, h, b], row_recv.at[t, odd, b], h)

    def row_sent(t, b=0):
        for h in range(2):
            src, dst = row_refs(t, h, b)
            row_wait_send(src, dst, row_send.at[t, h, b], row_recv.at[t, odd, b], h)

    def row_arrive(t, j, b=0):
        if t == 1:
            dst = qn.at[pl.ds(2 * j, 2)]
        elif t == 3:
            dst = don.at[pl.ds(2 * j, 2)]
        elif t == 4:
            dst = sel_land.at[j]
        else:
            dst = piece(t // 2, 0, c, j, b)
        row_wait_recv(dst, row_recv.at[t, j, b])

    def piece(t, shift, core, j, b):
        quarter = lax.rem(y + shift + ROW, ROW)
        return (kn, vn)[t].at[pl.ds(4 * (2 * quarter + core) + 2 * j + b, 1)]

    def kv_sib(t, m, j, b):
        own = piece(t, SHIFTS[m], c, j, b)
        return remote(
            own, own, kv_sib_send.at[t, m, j, b], kv_sib_recv.at[t, m, j, b], sibling
        )

    def kv_ring(t, way, j, b):
        own = piece(t, 0, c, j, b)
        return remote(
            own, own, kv_send.at[t, way, j, b], kv_recv.at[t, way, j, b], (up, down)[way]
        )

    def kv_far(t, way, b):
        own = piece(t, (-1, 1)[way], c, way, b)
        return remote(
            own, own, kv_far_send.at[t, way, b], kv_far_recv.at[t, way, b], (up, down)[way]
        )

    def kv_begin(t, b):
        for j in range(2):
            row_arrive(2 * t, j, b)
            kv_ring(t, j, j, b).start()
            kv_ring(t, 1 - j, j, b).start()
            kv_sib(t, 0, j, b).start()

    def kv_relay(t, b):
        for way in range(2):
            kv_ring(t, way, way, b).wait_recv()
            kv_far(t, way, b).start()
            kv_sib(t, 1 + way, way, b).start()

    def kv_rest(t, b):
        for way in range(2):
            kv_ring(t, way, 1 - way, b).wait_recv()
            kv_sib(t, 1 + way, 1 - way, b).start()

    def kv_last(t, b):
        for way in range(2):
            kv_far(t, way, b).wait_recv()
            kv_sib(t, 3, way, b).start()

    def kv_end(t):
        for m in range(4):
            for j in range(2):
                for b in range(2):
                    kv_sib(t, m, j, b).wait_recv()

    def gradient_rows(lo, hi):
        @pl.loop(lo, hi)
        def _(i):
            rows = pl.ds(pl.multiple_of((i % 2) * 256, 256), 256)
            tile = dot(cot[i // 2, rows, :], weight[...], ((1,), (1,)))
            k_own[i // 2, rows, :] = tile.astype(bf16)

    out, dq = don, scaled

    def item_block(item):
        return 8 * y + 4 * c + item

    def chosen_id(item, t):
        return sel[item // 2, item % 2, t - 1]

    def slot_id(item, t):
        return jnp.where(t == 0, item_block(item), chosen_id(item, jnp.maximum(t, 1)))

    def weigh(lo, hi):
        @pl.loop(lo, hi)
        def _(item):
            block = item_block(item)
            query_t = qn[item].T

            def keep(s, t):
                for n in range(ITEMS):
                    terms[n, t] = s[:, n * HEAD : (n + 1) * HEAD]
                return jnp.max(s, axis=0, keepdims=True)

            s = dot(kn[block], query_t, ((1,), (0,)))
            key_at = lax.broadcasted_iota(jnp.int32, (BLOCK, BLOCK), 0)
            query_at = lax.broadcasted_iota(jnp.int32, (BLOCK, BLOCK), 1)
            top = keep(jnp.where(key_at <= query_at, s, -1e30), 0)

            def score(t, top):
                at = chosen_id(item, t)
                s = dot(kn[at], query_t, ((1,), (0,)))
                return jnp.maximum(top, keep(jnp.where(at < block, s, -1e30), t))

            top = lax.fori_loop(1, SLOTS, score, top) * FACTOR

            def exponentiate(t, total):
                sums = []
                for n in range(ITEMS):
                    cols = slice(n * HEAD, (n + 1) * HEAD)
                    e = jnp.exp2(terms[n, t] * FACTOR - top[:, cols])
                    sums.append(jnp.sum(e, axis=0, keepdims=True))
                    expons[item, t, :, cols] = e.astype(bf16)
                return total + jnp.concatenate(sums, axis=1)

            stats[item] = 1.0 / lax.fori_loop(
                0, SLOTS, exponentiate, jnp.zeros((1, BLOCK), f32)
            )

    def value_terms():
        @pl.loop(0, ITEMS)
        def _(item):
            scaled_t = (don[item].T.astype(f32) * stats[item]).astype(bf16)
            scaled[item] = scaled_t.T

            @pl.loop(0, SLOTS)
            def _(t):
                terms[item, t] = dot(expons[item, t], scaled[item], ((1,), (0,)))

    def attend():
        @pl.loop(0, ITEMS)
        def _(item):
            def add(t, out_t):
                return out_t + dot(vn[slot_id(item, t)], expons[item, t], ((0,), (0,)))

            out_t = lax.fori_loop(0, SLOTS, add, jnp.zeros((HEAD, BLOCK), f32))
            out_t = (out_t * stats[item]).astype(bf16)
            product = don[item].T.astype(f32) * out_t.astype(f32)
            out[item] = out_t.T
            stats[item] = jnp.sum(product, axis=0, keepdims=True) * stats[item]

    def backward(lo, hi):
        @pl.loop(lo, hi)
        def _(item):
            query = qn[item]
            scaled_t = scaled[item].T
            delta = stats[item]

            def add(t, dq_t):
                at = slot_id(item, t)
                for n in range(BLOCK // STEP):
                    rows = slice(n * STEP, (n + 1) * STEP)
                    dp = dot(vn[at, rows, :], scaled_t, ((1,), (0,)))
                    ds = (expons[item, t, rows, :].astype(f32) * (dp - delta)).astype(bf16)
                    dq_t = dq_t + dot(kn[at, rows, :], ds, ((0,), (0,)))
                    terms[item, t, rows, :] = dot(ds, query, ((1,), (0,)))
                return dq_t

            dq_t = lax.fori_loop(0, SLOTS, add, jnp.zeros((HEAD, BLOCK), f32), unroll=True)
            dq[item] = (dq_t * SCALING).astype(bf16).T

    def gather_terms(t, m):
        @pl.loop(0, 8)
        def _(i):
            target = 8 * lax.rem(y + SHIFTS[m] + ROW, ROW) + i
            total = jnp.zeros((BLOCK, HEAD), f32)
            for item in range(ITEMS):
                block = item_block(item)
                slot = jnp.int32(0)
                for s in range(1, SLOTS):
                    slot = jnp.where(chosen_id(item, s) == target, s, slot)
                slot = jnp.where(target == block, 0, slot)
                chosen = (target == block) | (slot > 0)
                total = total + jnp.where(chosen, terms[item, slot], 0.0)
            if t == 0:
                total = total * SCALING
            parts[t, m, i // 4, i % 4] = total.astype(bf16)

    homes = (dk_home, dv_home, dq_home, attn)
    sources = (parts.at[0, 0, c], parts.at[1, 0, c], dq, out)

    def home_refs(t, j):
        cols = pl.ds(pl.multiple_of(odd * HEAD, HEAD), HEAD)
        return sources[t].at[pl.ds(2 * j, 2)], homes[t].at[:, :, cols]

    def go_home(t, j):
        src, dst = home_refs(t, j)
        row_start(src, dst, home_send.at[t, j], home_recv.at[t, odd], j)

    def come_home(t):
        for h in range(2):
            row_wait_recv(homes[t].at[:, :, pl.ds(h * HEAD, HEAD)], home_recv.at[t, h])

    def sib_copy(t, m):
        return remote(
            parts.at[t, m, 1 - c], theirs.at[t, m],
            sib_send.at[t, m], sib_recv.at[t, m], sibling,
        )

    def far_copy(t, way):
        return remote(
            parts.at[t, 3, c, pl.ds(2 * way, 2)], far.at[t, way],
            far_send.at[t, way], far_recv.at[t, way], (up, down)[way],
        )

    def ring_copy(t, way, j):
        return remote(
            parts.at[t, 2 - way, c, pl.ds(2 * j, 2)], near.at[t, way, j],
            ring_send.at[t, way, j], ring_recv.at[t, way, j], (up, down)[way],
        )

    def share(t, *shifts):
        for m in shifts:
            gather_terms(t, m)
            sib_copy(t, m).start()

    def add_theirs(t, m):
        sib_copy(t, m).wait_recv()

        @pl.loop(0, 4)
        def _(i):
            total = parts[t, m, c, i].astype(f32) + theirs[t, m, i].astype(f32)
            parts[t, m, c, i] = total.astype(bf16)

    def back_far(t):
        add_theirs(t, 3)
        for way in range(2):
            far_copy(t, way).start()

    def back_near(t):
        for way in range(2):
            add_theirs(t, 2 - way)
            ring_copy(t, way, 1 - way).start()

    def back_sum(t):
        for way in range(2):
            far_copy(t, way).wait_recv()

            @pl.loop(0, 2)
            def _(i, way=way):
                total = parts[t, 2 - way, c, 2 * way + i].astype(f32)
                total = total + far[t, way, i].astype(f32)
                parts[t, 2 - way, c, 2 * way + i] = total.astype(bf16)

            ring_copy(t, way, way).start()

    def back_end(t):
        sib_copy(t, 0).wait_recv()
        for j in range(2):
            for way in range(2):
                ring_copy(t, way, j).wait_recv()

            @pl.loop(0, 2)
            def _(i, j=j):
                total = parts[t, 0, c, 2 * j + i].astype(f32)
                total = total + theirs[t, 0, 2 * j + i].astype(f32)
                total = total + near[t, 0, j, i].astype(f32)
                total = total + near[t, 1, j, i].astype(f32)
                parts[t, 0, c, 2 * j + i] = total.astype(bf16)

            go_home(t, j)

    def part_copy():
        return remote(part.at[:, 1 - c], part_sib, part_send, part_recv, sibling)

    def z_at(shift):
        return lax.rem(z + shift + DEPTH, DEPTH)

    def z_copy(way, step):
        src = part.at[z_at(step if way == 0 else -step), c]
        dst = part_in.at[way, step - 1]
        if step == DEPTH // 2:
            rows = pl.ds(way * (CHUNK // 2), CHUNK // 2)
            src, dst = src.at[rows], dst.at[rows]
        return remote(
            src, dst, z_send.at[way, step - 1], z_recv.at[way, step - 1], (z_next, z_last)[way]
        )

    def z_step(step):
        for way in range(2):
            z_copy(way, step + 1).wait_recv()
            mine_at = z_at(step if way == 0 else -step)
            rows = pl.ds(0, CHUNK)
            if step + 1 == DEPTH // 2:
                rows = pl.ds(way * (CHUNK // 2), CHUNK // 2)
            total = part[mine_at, c, rows, :].astype(f32)
            total = total + part_in[way, step, rows, :].astype(f32)
            part[mine_at, c, rows, :] = total.astype(bf16)
            z_copy(way, step).start()

    def project():
        @pl.loop(0, 4)
        def _(i):
            rows = pl.ds(pl.multiple_of((i % 2) * 256, 256), 256)
            for n in range(4):
                cols = pl.ds(n * 512, 512)
                tile = dot(attn[i // 2, rows, :], weight[:, cols], ((1,), (0,))).astype(bf16)
                for a in range(2):
                    for b in range(2):
                        at = (2 * a + b) * CHUNK
                        part[2 * i + a, b, :, cols] = tile[at : at + CHUNK, :]

        part_copy().start()

    def project_sum():
        part_copy().wait()

        @pl.loop(0, DEPTH)
        def _(i):
            total = part[i, c].astype(f32) + part_sib[i].astype(f32)
            part[i, c] = total.astype(bf16)

        for way in range(2):
            z_copy(way, DEPTH // 2).start()

    def project_end():
        total = part[z, c].astype(f32)
        for way in range(2):
            z_copy(way, 1).wait_recv()
            total = total + part_in[way, 0].astype(f32)
        projected[...] = total.astype(bf16)

    def across_copy(d):
        return remote(
            chunks.at[lax.rem(x + d, ROW)], row_in.at[d - 1],
            wx_send.at[d - 1], wx_recv.at[d - 1], across[d - 1],
        )

    def along_copy(d):
        return remote(
            chunk_sum.at[lax.rem(y + d, ROW)], col_in.at[d - 1],
            wy_send.at[d - 1], wy_recv.at[d - 1], along[d - 1],
        )

    def weight_start():
        first_t, second_t = attn[0].T, attn[1].T
        for yy in range(ROW):
            cols = slice(yy * 512, (yy + 1) * 512)
            tile = dot(first_t, cot[0, :, cols], ((1,), (0,)))
            tile = tile + dot(second_t, cot[1, :, cols], ((1,), (0,)))
            for xx in range(ROW):
                chunks[xx, yy] = tile[:, xx * 128 : (xx + 1) * 128].astype(bf16)
        for d in range(1, ROW):
            across_copy(d).start()

    def weight_middle():
        for d in range(1, ROW):
            across_copy(d).wait_recv()
        for yy in range(ROW):
            total = chunks[x, yy].astype(f32)
            for d in range(ROW - 1):
                total = total + row_in[d, yy].astype(f32)
            chunk_sum[yy] = total.astype(bf16)
        for d in range(1, ROW):
            along_copy(d).start()

    def weight_end():
        total = chunk_sum[y].astype(f32)
        for d in range(1, ROW):
            along_copy(d).wait_recv()
            total = total + col_in[d - 1].astype(f32)
        weight_grad[...] = total

    loads[0].wait()
    row_go(0, 0)
    loads[1].wait()
    row_sent(0, 0)
    row_go(0, 1)
    kv_begin(0, 0)
    row_sent(0, 1)
    row_go(2, 0)
    kv_begin(0, 1)
    loads[2].wait()
    loads[3].wait()
    gradient_rows(0, 2)
    kv_relay(0, 0)
    row_sent(2, 0)
    row_go(2, 1)
    gradient_rows(2, 4)
    kv_relay(0, 1)
    kv_rest(0, 0)
    row_sent(2, 1)
    row_go(1)
    row_go(4)
    kv_rest(0, 1)
    kv_last(0, 0)
    kv_begin(1, 0)
    row_sent(1)
    row_go(3)
    kv_last(0, 1)
    kv_begin(1, 1)
    for j in range(2):
        row_arrive(4, j)
    sel_copy = pltpu.make_async_copy(sel_land, sel, sel_sem)
    sel_copy.start()
    for j in range(2):
        row_arrive(1, j)
    kv_end(0)
    sel_copy.wait()
    weigh(0, 3)
    kv_relay(1, 0)
    kv_relay(1, 1)
    weigh(3, 4)
    kv_rest(1, 0)
    kv_rest(1, 1)
    for j in range(2):
        row_arrive(3, j)
    value_terms()
    share(1, 3, 1)
    back_far(1)
    share(1, 2, 0)
    kv_last(1, 0)
    kv_last(1, 1)
    kv_end(1)
    attend()
    for j in range(2):
        go_home(3, j)
    back_near(1)
    backward(0, 2)
    go_home(2, 0)
    back_sum(1)
    come_home(3)
    project()
    backward(2, 3)
    project_sum()
    backward(3, 4)
    go_home(2, 1)
    share(0, 3, 1)
    back_far(0)
    share(0, 2, 0)
    z_step(3)
    back_near(0)
    back_end(1)
    weight_start()
    z_step(2)
    back_sum(0)
    z_step(1)
    back_end(0)
    weight_middle()
    project_end()
    weight_end()

    for t in range(3):
        come_home(t)
    row_sent(3)
    row_sent(4)
    for t in range(4):
        for j in range(2):
            src, dst = home_refs(t, j)
            row_wait_send(src, dst, home_send.at[t, j], home_recv.at[t, odd], j)
    for t in range(2):
        for m in range(4):
            sib_copy(t, m).wait_send()
            for j in range(2):
                for b in range(2):
                    kv_sib(t, m, j, b).wait_send()
        for way in range(2):
            far_copy(t, way).wait_send()
            for j in range(2):
                ring_copy(t, way, j).wait_send()
                kv_far(t, way, j).wait_send()
                for b in range(2):
                    kv_ring(t, way, j, b).wait_send()
    for step in range(1, DEPTH // 2 + 1):
        for way in range(2):
            z_copy(way, step).wait_send()
    for d in range(1, ROW):
        across_copy(d).wait_send()
        along_copy(d).wait_send()


def layer(q, k, v, sel, weight, cot):
    f32, bf16 = jnp.float32, jnp.bfloat16
    home = jax.ShapeDtypeStruct((2, BLOCK, 2 * HEAD), bf16)
    dma = pltpu.SemaphoreType.DMA
    vmem = pl.BlockSpec(memory_space=pltpu.VMEM)
    wide = weight.shape[1]
    own = pltpu.VMEM((2, BLOCK, 2 * HEAD), bf16)
    eighth = pltpu.VMEM((ITEMS, BLOCK, HEAD), bf16)
    return pl.pallas_call(
        layer_kernel,
        name="layer",
        out_shape=(
            jax.ShapeDtypeStruct((CHUNK, wide), bf16),
            home, home, home,
            jax.ShapeDtypeStruct((2 * HEAD, HEAD), f32),
            jax.ShapeDtypeStruct(sel.shape, jnp.int32),
        ),
        in_specs=[ANY] * 6,
        out_specs=(vmem, ANY, ANY, ANY, vmem, ANY),
        scratch_shapes=[
            own, own,
            pltpu.VMEM(weight.shape, bf16),
            pltpu.VMEM((2, BLOCK, wide), bf16),
            pltpu.SMEM(sel.shape, jnp.int32),
            eighth,
            pltpu.VMEM((ALL_BLOCKS, BLOCK, HEAD), bf16),
            pltpu.VMEM((ALL_BLOCKS, BLOCK, HEAD), bf16),
            eighth, eighth,
            pltpu.VMEM((ITEMS, SLOTS, BLOCK, BLOCK), bf16),
            pltpu.VMEM((ITEMS, SLOTS, BLOCK, HEAD), f32),
            pltpu.VMEM((ITEMS, 1, BLOCK), f32),
            pltpu.VMEM((2, 4, 2, 4, BLOCK, HEAD), bf16),
            pltpu.VMEM((2, 4, 4, BLOCK, HEAD), bf16),
            pltpu.VMEM((2, 2, 2, 2, BLOCK, HEAD), bf16),
            pltpu.VMEM((2, 2, 2, BLOCK, HEAD), bf16),
            own,
            pltpu.VMEM((DEPTH, 2, CHUNK, wide), bf16),
            pltpu.VMEM((DEPTH, CHUNK, wide), bf16),
            pltpu.VMEM((2, DEPTH // 2, CHUNK, wide), bf16),
            pltpu.VMEM((ROW, ROW, 2 * HEAD, HEAD), bf16),
            pltpu.VMEM((ROW, 2 * HEAD, HEAD), bf16),
            pltpu.VMEM((ROW - 1, ROW, 2 * HEAD, HEAD), bf16),
            pltpu.VMEM((ROW - 1, 2 * HEAD, HEAD), bf16),
            dma((4,)), dma, dma((5, 2, 2)), dma((5, 2, 2)),
            dma((2, 2, 2, 2)), dma((2, 2, 2, 2)), dma((2, 2, 2)), dma((2, 2, 2)),
            dma((2, 4, 2, 2)), dma((2, 4, 2, 2)), dma((4, 2)), dma((4, 2)),
            dma((2, 4)), dma((2, 4)), dma((2, 2, 2)), dma((2, 2, 2)), dma((2, 2)), dma((2, 2)),
            dma, dma, dma((2, 4)), dma((2, 4)), dma((3,)), dma((3,)), dma((3,)), dma((3,)),
        ],
        compiler_params=pltpu.CompilerParams(
            collective_id=0, has_side_effects=True, vmem_limit_bytes=VMEM_LIMIT
        ),
    )(q, k, v, sel, weight, cot)


def settle_kernel(*refs):
    count = len(refs) // 2
    for i in range(count):
        refs[count + i][...] = refs[i][...]


def settle(*arrays):
    vmem = pl.BlockSpec(memory_space=pltpu.VMEM)
    return pl.pallas_call(
        settle_kernel,
        name="settle",
        out_shape=tuple(jax.ShapeDtypeStruct(a.shape, a.dtype) for a in arrays),
        in_specs=[vmem] * len(arrays),
        out_specs=(vmem,) * len(arrays),
        compiler_params=pltpu.CompilerParams(vmem_limit_bytes=VMEM_LIMIT),
    )(*arrays)


def shards(queries, key_states, values, selection, out_weight, cotangent):
    def blocks(array):
        return array.reshape(2, BLOCK, -1)

    results = layer(
        blocks(queries), blocks(key_states), blocks(values), selection, out_weight,
        blocks(cotangent),
    )
    projected, query_grad, key_grad, value_grad, weight_grad = settle(*results[:5])
    query_grad, key_grad, value_grad = (
        g.reshape(queries.shape) for g in (query_grad, key_grad, value_grad)
    )
    return projected, query_grad, key_grad, value_grad, weight_grad


def solution(mesh):
    in_specs = (
        P("seq", "head"),
        P("seq", "head"),
        P("seq", "head"),
        P("head", "seq", None),
        P("head", None),
        P("seq", None),
    )
    out_specs = (
        P(("seq", "head"), None),
        P("seq", "head"),
        P("seq", "head"),
        P("seq", "head"),
        P("head", "seq"),
    )
    return jax.shard_map(shards, mesh=mesh, in_specs=in_specs, out_specs=out_specs, check_vma=False)
```

```python
import math

import jax
import jax.numpy as jnp
from jax import lax
from jax.experimental import pallas as pl
from jax.experimental.pallas import tpu as pltpu
from jax.sharding import PartitionSpec as P

ROW = 4
DEPTH = 8
HEAD = 128
BLOCK = 512
ITEMS = 4
SLOTS = 5
ALL_BLOCKS = 32
CHUNK = 64
STEP = 256
SHIFTS = (0, -1, 1, 2)
SCALING = 1.0 / math.sqrt(HEAD)
FACTOR = SCALING * math.log2(math.e)
MESH = pl.DeviceIdType.MESH
VMEM_LIMIT = 62 * 1024 * 1024
ANY = pl.BlockSpec(memory_space=pl.ANY)


def place():
    seq = lax.axis_index("seq")
    head = lax.axis_index("head")
    return seq // ROW, seq % ROW, head // 2, head % 2


def remote(src, dst, send_sem, recv_sem, device):
    return pltpu.make_async_remote_copy(
        src_ref=src,
        dst_ref=dst,
        send_sem=send_sem,
        recv_sem=recv_sem,
        device_id=device,
        device_id_type=MESH,
    )


def row_partner(k):
    y, x, z, c = place()
    device = (y * ROW + 2 * c + k, 2 * z + x // 2)
    return device, (x // 2 == c) & (x % 2 == k)


def row_start(src, dst, send_sem, recv_sem, k):
    device, own = row_partner(k)

    @pl.when(jnp.logical_not(own))
    def _():
        remote(src, dst, send_sem, recv_sem, device).start()

    @pl.when(own)
    def _():
        pltpu.make_async_copy(src, dst, recv_sem).start()


def row_wait_recv(dst, recv_sem):
    pltpu.make_async_copy(dst, dst, recv_sem).wait()


def row_wait_send(src, dst, send_sem, recv_sem, k):
    device, own = row_partner(k)

    @pl.when(jnp.logical_not(own))
    def _():
        remote(src, dst, send_sem, recv_sem, device).wait_send()


def meet(others):
    y, x, z, c = place()
    barrier = pltpu.get_barrier_semaphore()
    for k in range(2):
        device, own = row_partner(k)

        @pl.when(jnp.logical_not(own))
        def _(device=device):
            pl.semaphore_signal(barrier, inc=1, device_id=device, device_id_type=MESH)

    for device in others:
        pl.semaphore_signal(barrier, inc=1, device_id=device, device_id_type=MESH)
    pl.semaphore_wait(barrier, 2 - (x // 2 == c).astype(jnp.int32) + len(others))


def dot(a, b, contract):
    return lax.dot_general(a, b, (contract, ((), ())), preferred_element_type=jnp.float32)


def layer_kernel(
    q_in, k_in, v_in, sel_in, weight_in, cot_in,
    projected, dq_home, dk_home, dv_home, weight_grad, sel_land,
    k_own, v_own, weight, cot, sel, qn, kn, vn, don, scaled, expons, terms, stats,
    parts, theirs, near, far, attn, part, part_sib, part_in, chunks, chunk_sum, row_in, col_in,
    load, sel_sem, row_send, row_recv, kv_send, kv_recv, kv_far_send, kv_far_recv,
    kv_sib_send, kv_sib_recv, home_send, home_recv, sib_send, sib_recv,
    ring_send, ring_recv, far_send, far_recv,
    part_send, part_recv, z_send, z_recv, wx_send, wx_recv, wy_send, wy_recv,
):
    y, x, z, c = place()
    odd = x % 2
    f32, bf16 = jnp.float32, jnp.bfloat16
    up = (lax.rem(y + 1, ROW) * ROW + x, 2 * z + c)
    down = (lax.rem(y + ROW - 1, ROW) * ROW + x, 2 * z + c)
    sibling = (y * ROW + x, 2 * z + 1 - c)
    z_next = (y * ROW + x, 2 * lax.rem(z + 1, DEPTH) + c)
    z_last = (y * ROW + x, 2 * lax.rem(z + DEPTH - 1, DEPTH) + c)
    across = [(y * ROW + lax.rem(x + d, ROW), 2 * z + c) for d in range(1, ROW)]
    along = [(lax.rem(y + d, ROW) * ROW + x, 2 * z + c) for d in range(1, ROW)]

    loads = [
        pltpu.make_async_copy(src, dst, load.at[i])
        for i, (src, dst) in enumerate(
            ((k_in, k_own), (v_in, v_own), (cot_in, cot), (weight_in, weight))
        )
    ]
    for copy in loads:
        copy.start()
    meet([up, down, sibling, z_next, z_last, along[1]] + across)

    home_at = 4 * (2 * y + x // 2) + 2 * odd

    def row_refs(t, h, b):
        cols = pl.ds(h * HEAD, HEAD)
        if t == 0:
            return k_own.at[pl.ds(b, 1), :, cols], kn.at[pl.ds(home_at + b, 1)]
        if t == 1:
            return q_in.at[:, :, cols], qn.at[pl.ds(2 * odd, 2)]
        if t == 2:
            return v_own.at[pl.ds(b, 1), :, cols], vn.at[pl.ds(home_at + b, 1)]
        if t == 3:
            return k_own.at[:, :, cols], don.at[pl.ds(2 * odd, 2)]
        return sel_in.at[h], sel_land.at[odd]

    def row_go(t, b=0):
        for h in range(2):
            src, dst = row_refs(t, h, b)
            row_start(src, dst, row_send.at[t, h, b], row_recv.at[t, odd, b], h)

    def row_sent(t, b=0):
        for h in range(2):
            src, dst = row_refs(t, h, b)
            row_wait_send(src, dst, row_send.at[t, h, b], row_recv.at[t, odd, b], h)

    def row_arrive(t, j, b=0):
        if t == 1:
            dst = qn.at[pl.ds(2 * j, 2)]
        elif t == 3:
            dst = don.at[pl.ds(2 * j, 2)]
        elif t == 4:
            dst = sel_land.at[j]
        else:
            dst = piece(t // 2, 0, c, j, b)
        row_wait_recv(dst, row_recv.at[t, j, b])

    def piece(t, shift, core, j, b):
        quarter = lax.rem(y + shift + ROW, ROW)
        return (kn, vn)[t].at[pl.ds(4 * (2 * quarter + core) + 2 * j + b, 1)]

    def kv_sib(t, m, j, b):
        own = piece(t, SHIFTS[m], c, j, b)
        return remote(
            own, own, kv_sib_send.at[t, m, j, b], kv_sib_recv.at[t, m, j, b], sibling
        )

    def kv_ring(t, way, j, b):
        own = piece(t, 0, c, j, b)
        return remote(
            own, own, kv_send.at[t, way, j, b], kv_recv.at[t, way, j, b], (up, down)[way]
        )

    def kv_far(t, way, b):
        own = piece(t, (-1, 1)[way], c, way, b)
        return remote(
            own, own, kv_far_send.at[t, way, b], kv_far_recv.at[t, way, b], (up, down)[way]
        )

    def kv_begin(t, b):
        for j in range(2):
            row_arrive(2 * t, j, b)
            kv_ring(t, j, j, b).start()
            kv_ring(t, 1 - j, j, b).start()
            kv_sib(t, 0, j, b).start()

    def kv_relay(t, b):
        for way in range(2):
            kv_ring(t, way, way, b).wait_recv()
            kv_far(t, way, b).start()
            kv_sib(t, 1 + way, way, b).start()

    def kv_rest(t, b):
        for way in range(2):
            kv_ring(t, way, 1 - way, b).wait_recv()
            kv_sib(t, 1 + way, 1 - way, b).start()

    def kv_last(t, b):
        for way in range(2):
            kv_far(t, way, b).wait_recv()
            kv_sib(t, 3, way, b).start()

    def kv_end(t):
        for m in range(4):
            for j in range(2):
                for b in range(2):
                    kv_sib(t, m, j, b).wait_recv()

    def gradient_rows(lo, hi):
        @pl.loop(lo, hi)
        def _(i):
            rows = pl.ds(pl.multiple_of((i % 2) * 256, 256), 256)
            tile = dot(cot[i // 2, rows, :], weight[...], ((1,), (1,)))
            k_own[i // 2, rows, :] = tile.astype(bf16)

    out, dq = don, scaled

    def item_block(item):
        return 8 * y + 4 * c + item

    def chosen_id(item, t):
        return sel[item // 2, item % 2, t - 1]

    def slot_id(item, t):
        return jnp.where(t == 0, item_block(item), chosen_id(item, jnp.maximum(t, 1)))

    def weigh(lo, hi):
        @pl.loop(lo, hi)
        def _(item):
            block = item_block(item)
            query_t = qn[item].T

            def keep(s, t):
                for n in range(ITEMS):
                    terms[n, t] = s[:, n * HEAD : (n + 1) * HEAD]
                return jnp.max(s, axis=0, keepdims=True)

            s = dot(kn[block], query_t, ((1,), (0,)))
            key_at = lax.broadcasted_iota(jnp.int32, (BLOCK, BLOCK), 0)
            query_at = lax.broadcasted_iota(jnp.int32, (BLOCK, BLOCK), 1)
            top = keep(jnp.where(key_at <= query_at, s, -1e30), 0)

            def score(t, top):
                at = chosen_id(item, t)
                s = dot(kn[at], query_t, ((1,), (0,)))
                return jnp.maximum(top, keep(jnp.where(at < block, s, -1e30), t))

            top = lax.fori_loop(1, SLOTS, score, top) * FACTOR

            def exponentiate(t, total):
                sums = []
                for n in range(ITEMS):
                    cols = slice(n * HEAD, (n + 1) * HEAD)
                    e = jnp.exp2(terms[n, t] * FACTOR - top[:, cols])
                    sums.append(jnp.sum(e, axis=0, keepdims=True))
                    expons[item, t, :, cols] = e.astype(bf16)
                return total + jnp.concatenate(sums, axis=1)

            stats[item] = 1.0 / lax.fori_loop(
                0, SLOTS, exponentiate, jnp.zeros((1, BLOCK), f32)
            )

    def value_terms():
        @pl.loop(0, ITEMS)
        def _(item):
            scaled_t = (don[item].T.astype(f32) * stats[item]).astype(bf16)
            scaled[item] = scaled_t.T

            @pl.loop(0, SLOTS, unroll=True)
            def _(t):
                terms[item, t] = dot(expons[item, t], scaled[item], ((1,), (0,)))

    def attend():
        @pl.loop(0, ITEMS)
        def _(item):
            def add(t, out_t):
                return out_t + dot(vn[slot_id(item, t)], expons[item, t], ((0,), (0,)))

            out_t = lax.fori_loop(0, SLOTS, add, jnp.zeros((HEAD, BLOCK), f32), unroll=True)
            out_t = (out_t * stats[item]).astype(bf16)
            product = don[item].T.astype(f32) * out_t.astype(f32)
            out[item] = out_t.T
            stats[item] = jnp.sum(product, axis=0, keepdims=True) * stats[item]

    def backward(lo, hi):
        @pl.loop(lo, hi)
        def _(item):
            query = qn[item]
            scaled_t = scaled[item].T
            delta = stats[item]

            def add(t, dq_t):
                at = slot_id(item, t)
                for n in range(BLOCK // STEP):
                    rows = slice(n * STEP, (n + 1) * STEP)
                    dp = dot(vn[at, rows, :], scaled_t, ((1,), (0,)))
                    ds = (expons[item, t, rows, :].astype(f32) * (dp - delta)).astype(bf16)
                    dq_t = dq_t + dot(kn[at, rows, :], ds, ((0,), (0,)))
                    terms[item, t, rows, :] = dot(ds, query, ((1,), (0,)))
                return dq_t

            dq_t = lax.fori_loop(0, SLOTS, add, jnp.zeros((HEAD, BLOCK), f32), unroll=True)
            dq[item] = (dq_t * SCALING).astype(bf16).T

    def gather_terms(t, m):
        @pl.loop(0, 8)
        def _(i):
            target = 8 * lax.rem(y + SHIFTS[m] + ROW, ROW) + i
            total = jnp.zeros((BLOCK, HEAD), f32)
            for item in range(ITEMS):
                block = item_block(item)
                slot = jnp.int32(0)
                for s in range(1, SLOTS):
                    slot = jnp.where(chosen_id(item, s) == target, s, slot)
                slot = jnp.where(target == block, 0, slot)
                chosen = (target == block) | (slot > 0)
                total = total + jnp.where(chosen, terms[item, slot], 0.0)
            if t == 0:
                total = total * SCALING
            parts[t, m, i // 4, i % 4] = total.astype(bf16)

    homes = (dk_home, dv_home, dq_home, attn)
    sources = (parts.at[0, 0, c], parts.at[1, 0, c], dq, out)

    def home_refs(t, j):
        cols = pl.ds(pl.multiple_of(odd * HEAD, HEAD), HEAD)
        return sources[t].at[pl.ds(2 * j, 2)], homes[t].at[:, :, cols]

    def go_home(t, j):
        src, dst = home_refs(t, j)
        row_start(src, dst, home_send.at[t, j], home_recv.at[t, odd], j)

    def come_home(t):
        for h in range(2):
            row_wait_recv(homes[t].at[:, :, pl.ds(h * HEAD, HEAD)], home_recv.at[t, h])

    def sib_copy(t, m):
        return remote(
            parts.at[t, m, 1 - c], theirs.at[t, m],
            sib_send.at[t, m], sib_recv.at[t, m], sibling,
        )

    def far_copy(t, way):
        return remote(
            parts.at[t, 3, c, pl.ds(2 * way, 2)], far.at[t, way],
            far_send.at[t, way], far_recv.at[t, way], (up, down)[way],
        )

    def ring_copy(t, way, j):
        return remote(
            parts.at[t, 2 - way, c, pl.ds(2 * j, 2)], near.at[t, way, j],
            ring_send.at[t, way, j], ring_recv.at[t, way, j], (up, down)[way],
        )

    def share(t, *shifts):
        for m in shifts:
            gather_terms(t, m)
            sib_copy(t, m).start()

    def add_theirs(t, m):
        sib_copy(t, m).wait_recv()

        @pl.loop(0, 4)
        def _(i):
            total = parts[t, m, c, i].astype(f32) + theirs[t, m, i].astype(f32)
            parts[t, m, c, i] = total.astype(bf16)

    def back_far(t):
        add_theirs(t, 3)
        for way in range(2):
            far_copy(t, way).start()

    def back_near(t):
        for way in range(2):
            add_theirs(t, 2 - way)
            ring_copy(t, way, 1 - way).start()

    def back_sum(t):
        for way in range(2):
            far_copy(t, way).wait_recv()

            @pl.loop(0, 2)
            def _(i, way=way):
                total = parts[t, 2 - way, c, 2 * way + i].astype(f32)
                total = total + far[t, way, i].astype(f32)
                parts[t, 2 - way, c, 2 * way + i] = total.astype(bf16)

            ring_copy(t, way, way).start()

    def back_end(t):
        sib_copy(t, 0).wait_recv()
        for j in range(2):
            for way in range(2):
                ring_copy(t, way, j).wait_recv()

            @pl.loop(0, 2)
            def _(i, j=j):
                total = parts[t, 0, c, 2 * j + i].astype(f32)
                total = total + theirs[t, 0, 2 * j + i].astype(f32)
                total = total + near[t, 0, j, i].astype(f32)
                total = total + near[t, 1, j, i].astype(f32)
                parts[t, 0, c, 2 * j + i] = total.astype(bf16)

            go_home(t, j)

    def part_copy():
        return remote(part.at[:, 1 - c], part_sib, part_send, part_recv, sibling)

    def z_at(shift):
        return lax.rem(z + shift + DEPTH, DEPTH)

    def z_copy(way, step):
        src = part.at[z_at(step if way == 0 else -step), c]
        dst = part_in.at[way, step - 1]
        if step == DEPTH // 2:
            rows = pl.ds(way * (CHUNK // 2), CHUNK // 2)
            src, dst = src.at[rows], dst.at[rows]
        return remote(
            src, dst, z_send.at[way, step - 1], z_recv.at[way, step - 1], (z_next, z_last)[way]
        )

    def z_step(step):
        for way in range(2):
            z_copy(way, step + 1).wait_recv()
            mine_at = z_at(step if way == 0 else -step)
            rows = pl.ds(0, CHUNK)
            if step + 1 == DEPTH // 2:
                rows = pl.ds(way * (CHUNK // 2), CHUNK // 2)
            total = part[mine_at, c, rows, :].astype(f32)
            total = total + part_in[way, step, rows, :].astype(f32)
            part[mine_at, c, rows, :] = total.astype(bf16)
            z_copy(way, step).start()

    def project():
        @pl.loop(0, 4)
        def _(i):
            rows = pl.ds(pl.multiple_of((i % 2) * 256, 256), 256)
            for n in range(4):
                cols = pl.ds(n * 512, 512)
                tile = dot(attn[i // 2, rows, :], weight[:, cols], ((1,), (0,))).astype(bf16)
                for a in range(2):
                    for b in range(2):
                        at = (2 * a + b) * CHUNK
                        part[2 * i + a, b, :, cols] = tile[at : at + CHUNK, :]

        part_copy().start()

    def project_sum():
        part_copy().wait()

        @pl.loop(0, DEPTH)
        def _(i):
            total = part[i, c].astype(f32) + part_sib[i].astype(f32)
            part[i, c] = total.astype(bf16)

        for way in range(2):
            z_copy(way, DEPTH // 2).start()

    def project_end():
        total = part[z, c].astype(f32)
        for way in range(2):
            z_copy(way, 1).wait_recv()
            total = total + part_in[way, 0].astype(f32)
        projected[...] = total.astype(bf16)

    def across_copy(d):
        return remote(
            chunks.at[lax.rem(x + d, ROW)], row_in.at[d - 1],
            wx_send.at[d - 1], wx_recv.at[d - 1], across[d - 1],
        )

    def along_copy(d):
        return remote(
            chunk_sum.at[lax.rem(y + d, ROW)], col_in.at[d - 1],
            wy_send.at[d - 1], wy_recv.at[d - 1], along[d - 1],
        )

    def weight_start():
        first_t, second_t = attn[0].T, attn[1].T
        for yy in range(ROW):
            cols = slice(yy * 512, (yy + 1) * 512)
            tile = dot(first_t, cot[0, :, cols], ((1,), (0,)))
            tile = tile + dot(second_t, cot[1, :, cols], ((1,), (0,)))
            for xx in range(ROW):
                chunks[xx, yy] = tile[:, xx * 128 : (xx + 1) * 128].astype(bf16)
        for d in range(1, ROW):
            across_copy(d).start()

    def weight_middle():
        for d in range(1, ROW):
            across_copy(d).wait_recv()
        for yy in range(ROW):
            total = chunks[x, yy].astype(f32)
            for d in range(ROW - 1):
                total = total + row_in[d, yy].astype(f32)
            chunk_sum[yy] = total.astype(bf16)
        for d in range(1, ROW):
            along_copy(d).start()

    def weight_end():
        total = chunk_sum[y].astype(f32)
        for d in range(1, ROW):
            along_copy(d).wait_recv()
            total = total + col_in[d - 1].astype(f32)
        weight_grad[...] = total

    loads[0].wait()
    row_go(0, 0)
    loads[1].wait()
    row_sent(0, 0)
    row_go(0, 1)
    kv_begin(0, 0)
    row_sent(0, 1)
    row_go(2, 0)
    kv_begin(0, 1)
    loads[2].wait()
    loads[3].wait()
    gradient_rows(0, 2)
    kv_relay(0, 0)
    row_sent(2, 0)
    row_go(2, 1)
    gradient_rows(2, 4)
    kv_relay(0, 1)
    kv_rest(0, 0)
    row_sent(2, 1)
    row_go(1)
    row_go(4)
    kv_rest(0, 1)
    kv_last(0, 0)
    kv_begin(1, 0)
    row_sent(1)
    row_go(3)
    kv_last(0, 1)
    kv_begin(1, 1)
    for j in range(2):
        row_arrive(4, j)
    sel_copy = pltpu.make_async_copy(sel_land, sel, sel_sem)
    sel_copy.start()
    for j in range(2):
        row_arrive(1, j)
    kv_end(0)
    sel_copy.wait()
    weigh(0, 3)
    kv_relay(1, 0)
    kv_relay(1, 1)
    weigh(3, 4)
    kv_rest(1, 0)
    kv_rest(1, 1)
    for j in range(2):
        row_arrive(3, j)
    value_terms()
    share(1, 3, 1)
    back_far(1)
    share(1, 2, 0)
    kv_last(1, 0)
    kv_last(1, 1)
    kv_end(1)
    attend()
    for j in range(2):
        go_home(3, j)
    back_near(1)
    backward(0, 2)
    go_home(2, 0)
    back_sum(1)
    come_home(3)
    project()
    backward(2, 3)
    project_sum()
    backward(3, 4)
    go_home(2, 1)
    share(0, 3, 1)
    back_far(0)
    share(0, 2, 0)
    z_step(3)
    back_near(0)
    back_end(1)
    weight_start()
    z_step(2)
    back_sum(0)
    z_step(1)
    back_end(0)
    weight_middle()
    project_end()
    weight_end()

    for t in range(3):
        come_home(t)
    row_sent(3)
    row_sent(4)
    for t in range(4):
        for j in range(2):
            src, dst = home_refs(t, j)
            row_wait_send(src, dst, home_send.at[t, j], home_recv.at[t, odd], j)
    for t in range(2):
        for m in range(4):
            sib_copy(t, m).wait_send()
            for j in range(2):
                for b in range(2):
                    kv_sib(t, m, j, b).wait_send()
        for way in range(2):
            far_copy(t, way).wait_send()
            for j in range(2):
                ring_copy(t, way, j).wait_send()
                kv_far(t, way, j).wait_send()
                for b in range(2):
                    kv_ring(t, way, j, b).wait_send()
    for step in range(1, DEPTH // 2 + 1):
        for way in range(2):
            z_copy(way, step).wait_send()
    for d in range(1, ROW):
        across_copy(d).wait_send()
        along_copy(d).wait_send()


def layer(q, k, v, sel, weight, cot):
    f32, bf16 = jnp.float32, jnp.bfloat16
    home = jax.ShapeDtypeStruct((2, BLOCK, 2 * HEAD), bf16)
    dma = pltpu.SemaphoreType.DMA
    vmem = pl.BlockSpec(memory_space=pltpu.VMEM)
    wide = weight.shape[1]
    own = pltpu.VMEM((2, BLOCK, 2 * HEAD), bf16)
    eighth = pltpu.VMEM((ITEMS, BLOCK, HEAD), bf16)
    return pl.pallas_call(
        layer_kernel,
        name="layer",
        out_shape=(
            jax.ShapeDtypeStruct((CHUNK, wide), bf16),
            home, home, home,
            jax.ShapeDtypeStruct((2 * HEAD, HEAD), f32),
            jax.ShapeDtypeStruct(sel.shape, jnp.int32),
        ),
        in_specs=[ANY] * 6,
        out_specs=(vmem, ANY, ANY, ANY, vmem, ANY),
        scratch_shapes=[
            own, own,
            pltpu.VMEM(weight.shape, bf16),
            pltpu.VMEM((2, BLOCK, wide), bf16),
            pltpu.SMEM(sel.shape, jnp.int32),
            eighth,
            pltpu.VMEM((ALL_BLOCKS, BLOCK, HEAD), bf16),
            pltpu.VMEM((ALL_BLOCKS, BLOCK, HEAD), bf16),
            eighth, eighth,
            pltpu.VMEM((ITEMS, SLOTS, BLOCK, BLOCK), bf16),
            pltpu.VMEM((ITEMS, SLOTS, BLOCK, HEAD), f32),
            pltpu.VMEM((ITEMS, 1, BLOCK), f32),
            pltpu.VMEM((2, 4, 2, 4, BLOCK, HEAD), bf16),
            pltpu.VMEM((2, 4, 4, BLOCK, HEAD), bf16),
            pltpu.VMEM((2, 2, 2, 2, BLOCK, HEAD), bf16),
            pltpu.VMEM((2, 2, 2, BLOCK, HEAD), bf16),
            own,
            pltpu.VMEM((DEPTH, 2, CHUNK, wide), bf16),
            pltpu.VMEM((DEPTH, CHUNK, wide), bf16),
            pltpu.VMEM((2, DEPTH // 2, CHUNK, wide), bf16),
            pltpu.VMEM((ROW, ROW, 2 * HEAD, HEAD), bf16),
            pltpu.VMEM((ROW, 2 * HEAD, HEAD), bf16),
            pltpu.VMEM((ROW - 1, ROW, 2 * HEAD, HEAD), bf16),
            pltpu.VMEM((ROW - 1, 2 * HEAD, HEAD), bf16),
            dma((4,)), dma, dma((5, 2, 2)), dma((5, 2, 2)),
            dma((2, 2, 2, 2)), dma((2, 2, 2, 2)), dma((2, 2, 2)), dma((2, 2, 2)),
            dma((2, 4, 2, 2)), dma((2, 4, 2, 2)), dma((4, 2)), dma((4, 2)),
            dma((2, 4)), dma((2, 4)), dma((2, 2, 2)), dma((2, 2, 2)), dma((2, 2)), dma((2, 2)),
            dma, dma, dma((2, 4)), dma((2, 4)), dma((3,)), dma((3,)), dma((3,)), dma((3,)),
        ],
        compiler_params=pltpu.CompilerParams(
            collective_id=0, has_side_effects=True, vmem_limit_bytes=VMEM_LIMIT
        ),
    )(q, k, v, sel, weight, cot)


def settle_kernel(*refs):
    count = len(refs) // 2
    for i in range(count):
        refs[count + i][...] = refs[i][...]


def settle(*arrays):
    vmem = pl.BlockSpec(memory_space=pltpu.VMEM)
    return pl.pallas_call(
        settle_kernel,
        name="settle",
        out_shape=tuple(jax.ShapeDtypeStruct(a.shape, a.dtype) for a in arrays),
        in_specs=[vmem] * len(arrays),
        out_specs=(vmem,) * len(arrays),
        compiler_params=pltpu.CompilerParams(vmem_limit_bytes=VMEM_LIMIT),
    )(*arrays)


def shards(queries, key_states, values, selection, out_weight, cotangent):
    def blocks(array):
        return array.reshape(2, BLOCK, -1)

    results = layer(
        blocks(queries), blocks(key_states), blocks(values), selection, out_weight,
        blocks(cotangent),
    )
    projected, query_grad, key_grad, value_grad, weight_grad = settle(*results[:5])
    query_grad, key_grad, value_grad = (
        g.reshape(queries.shape) for g in (query_grad, key_grad, value_grad)
    )
    return projected, query_grad, key_grad, value_grad, weight_grad


def solution(mesh):
    in_specs = (
        P("seq", "head"),
        P("seq", "head"),
        P("seq", "head"),
        P("head", "seq", None),
        P("head", None),
        P("seq", None),
    )
    out_specs = (
        P(("seq", "head"), None),
        P("seq", "head"),
        P("seq", "head"),
        P("seq", "head"),
        P("head", "seq"),
    )
    return jax.shard_map(shards, mesh=mesh, in_specs=in_specs, out_specs=out_specs, check_vma=False)
```
